256 devices in a mesh: rows: 128 (over z, x, y), sub: 2 (over core).
Axes of the slice: x: 4, y: 4, z: 8, core: 2. Of those that a mesh axis runs over, the one named last changes fastest.
Arguments:
- positions: int32 [3, 65536], P(None, ('rows', 'sub')), may hold values from 0 to 19999
- right_side: float32 [32, 65536], P(None, ('rows', 'sub'))
- start_guess: float32 [32, 65536], P(None, ('rows', 'sub')), may hold values from -3 to 3
Outputs:
- solution: float32 [32, 65536], P(None, ('rows', 'sub'))
- residual: float32 [32, 65536], P(None, ('rows', 'sub'))
The draws below stay inside these ranges and needn't reach their ends.
All inputs are finite; a program needn't handle non-finite values.
Results may differ from the reference program's by a relative error of at most 0.02.
Values may be sent and summed in bfloat16 or wider, within the bound.
A program may use at most 128 MiB of HBM per device.

```python
import math
import jax
import jax.numpy as jnp
from jax import lax

RHS = 32
ITERS = 2
POINTS = 65536


def draw_right_side(key, part):
    key = jax.random.fold_in(key, 11)
    first_key = jax.random.fold_in(key, 0)
    values = jax.random.normal(first_key, (RHS, POINTS), jnp.float32)
    growth = 1.0 + 2.0 * jnp.arange(POINTS, dtype=jnp.float32) / POINTS
    return (values * growth[None, :]).astype(jnp.float32)


def with_ends(values, own_key, low, high):
    longest = values.shape.index(max(values.shape))
    spots = []
    for shift in (0, 1):
        where = [jax.random.randint(jax.random.fold_in(own_key, axis), (), 0, length) for axis, length in enumerate(values.shape)]
        where[longest] = (where[longest] + shift) % values.shape[longest]
        spots.append(tuple(where))
    return values.at[spots[0]].set(low).at[spots[1]].set(high)


def steps_of(stream_key, shape, cuts, smallest, largest):
    loudness, own = 1.0, jax.random.fold_in(stream_key, 6)
    for dim, blocks in cuts:
        heights = jnp.exp(jax.random.uniform(jax.random.fold_in(own, dim), (blocks,), jnp.float32, smallest / len(cuts), largest / len(cuts)))
        loudness = loudness * jnp.repeat(heights, shape[dim] // blocks).reshape([-1 if axis == dim else 1 for axis in range(len(shape))])
    return loudness


def normal_values(own_key, dims, scale, bound, pieces=(), kind=jnp.bfloat16):
    level = steps_of(own_key, dims, pieces, -0.22, 0.18) if pieces else 1.0
    result = jax.random.normal(own_key, dims, jnp.float32) * scale * level
    return jnp.minimum(jnp.maximum(result, -bound), bound).astype(kind)


def setup_inputs(seed: int = 0) -> dict:
    key_list = jax.random.split(jax.random.key(seed), 4)
    return {
        "positions": with_ends(jax.random.randint(key_list[0], (3, POINTS), 0, 20000), jax.random.fold_in(key_list[0], 1), 0, 19999).astype(jnp.int32),
        "right_side": draw_right_side(jax.random.fold_in(key_list[3], 71), 0),
        "start_guess": normal_values(key_list[2], (RHS, POINTS), 0.5, 3.0, ((1, 256),), jnp.float32),
    }


wave_scale = 9.0 / math.pi
ridge = 1.0

def to_metres(positions):
    return positions.astype(jnp.float32) * 0.001

def kernel_tile(column_coords, row_coords):
    squared = jnp.zeros((column_coords.shape[1], row_coords.shape[1]), jnp.float32)
    for component in range(3):
        offsets = column_coords[component][:, None] - row_coords[component][None, :]
        squared = squared + offsets * offsets
    return jnp.sinc(wave_scale * jnp.sqrt(squared)).astype(jnp.bfloat16)

def apply_operator(values_in, coords):
    values_bf = values_in.astype(jnp.bfloat16)
    block_rows = 512 if POINTS % 512 == 0 else POINTS
    starts = jnp.arange(POINTS // block_rows, dtype=jnp.int32) * block_rows

    def one_block(first_row):
        rows_here = lax.dynamic_slice_in_dim(coords, first_row, block_rows, 1)
        return jnp.dot(values_bf.astype(jnp.float32), kernel_tile(coords, rows_here).astype(jnp.float32), preferred_element_type=jnp.float32)
    blocks = lax.map(one_block, starts)
    product = jnp.transpose(blocks, (1, 0, 2)).reshape(values_in.shape[0], POINTS)
    return product + ridge * values_in

def gram(left, right):
    return jnp.dot(left, right.T, precision=lax.Precision.HIGHEST)

def spd_solve(matrix, targets):
    symmetric = 0.5 * (matrix + matrix.T)
    lower = jnp.linalg.cholesky(symmetric)
    return jax.scipy.linalg.cho_solve((lower, True), targets)

def reference(positions, right_side, start_guess):
    coords = to_metres(positions)
    solution = start_guess
    residual = right_side - apply_operator(start_guess, coords)
    direction = residual
    norm_now = gram(residual, residual)
    for iteration in range(ITERS):
        image = apply_operator(direction, coords)
        step_size = spd_solve(gram(direction, image), norm_now)
        solution = solution + jnp.dot(step_size.T, direction, precision=lax.Precision.HIGHEST)
        residual = residual - jnp.dot(step_size.T, image, precision=lax.Precision.HIGHEST)
        if iteration + 1 < ITERS:
            norm_next = gram(residual, residual)
            correction = spd_solve(norm_now, norm_next)
            direction = residual + jnp.dot(correction.T, direction, precision=lax.Precision.HIGHEST)
            norm_now = norm_next
    return (solution, residual)
```

```python
import jax
import jax.numpy as jnp
from jax import lax
from jax.experimental import pallas as pl
from jax.experimental.pallas import tpu as pltpu
from jax.sharding import PartitionSpec as P

MESH = pl.DeviceIdType.MESH
F32, BF16 = jnp.float32, jnp.bfloat16
HIGHEST = lax.Precision.HIGHEST

RHS = 32
OWN = 256
CHUNK = 2048
HALF = CHUNK // 2
QUARTER = CHUNK // 4
BOTH = 2 * OWN
FEATURES = 16
NZ, NA, NB = 8, 4, 4

SIGMA = (0.009 / (2.0 * 3.141592653589793)) ** 2
SCALE = -1.0 / 0.11181640625
SINE = (-0.1117412088270527, 0.7314446032490506, -1.3877725895638588)
ROUNDER = 12582912.0

ORDER = ((0, 0), (0, 1), (0, 3), (0, 2), (1, 0), (3, 0), (1, 1), (3, 1), (3, 3), (1, 3), (3, 2), (1, 2), (2, 0), (2, 3), (2, 1), (2, 2))
SLOT = {key: place for place, key in enumerate(ORDER)}
CHUNKS = len(ORDER)
GROUPS = (1, 2, 3, 5, 8, 12, 16)

SEMS = {}
for _name in (
    [("z", d) for d in range(1, NZ)]
    + [("b", 1), ("b", 3), ("b", 2, 0), ("b", 2, 1)]
    + [("a", d, db) for d in (1, 2, 3) for db in range(NB)]
    + ["part"]
):
    SEMS[_name] = len(SEMS)
N_SEMS = len(SEMS)
PHASES = (
    [(0, 0, d, 0) for d in range(1, NZ)],
    [(d, 0, 0, s) for d in range(4) for s in range(2) if d + s],
    [(0, d, 0, 0) for d in range(1, 4)],
)
SUM_SEM = {}
for _phase in PHASES:
    for _steps in _phase:
        SUM_SEM[_steps] = len(SUM_SEM)
N_SUM = len(SUM_SEM)


def dot_nt(left, right, precision=None):
    return lax.dot_general(left, right, (((1,), (1,)), ((), ())), precision=precision, preferred_element_type=F32)


def dot_tn(left, right, precision=HIGHEST):
    return lax.dot_general(left, right, (((0,), (0,)), ((), ())), precision=precision, preferred_element_type=F32)


def gram(left, right):
    return dot_nt(left, right, HIGHEST)


def packed(square):
    return jnp.concatenate([square[8 * k : 8 * k + 8] for k in range(4)], axis=1)


def unpacked(rows):
    return jnp.concatenate([rows[:, 32 * k : 32 * k + 32] for k in range(4)], axis=0)


def solve(*systems):
    where = lax.broadcasted_iota(jnp.int32, (RHS, 1), 0)
    work = [jnp.concatenate(pair, axis=1) * (1.0 / jnp.max(pair[0], axis=(0, 1), keepdims=True)) for pair in systems]
    for k in range(0, RHS, 2):
        for index, both in enumerate(work):
            top, low = both[k : k + 1, :], both[k + 1 : k + 2, :]
            a, b = top[:, k : k + 1], top[:, k + 1 : k + 2]
            c, d = low[:, k : k + 1], low[:, k + 1 : k + 2]
            inverse = 1.0 / (a * d - b * c)
            top, low = (d * inverse) * top - (b * inverse) * low, (a * inverse) * low - (c * inverse) * top
            rest = both - both[:, k : k + 1] * top - both[:, k + 1 : k + 2] * low
            work[index] = jnp.where(where == k, top, jnp.where(where == k + 1, low, rest))
    return [both[:, RHS:] for both in work]


def features(positions):
    centred = positions - 10000
    high = (centred + 64) >> 7
    low = centred - high * 128
    norm = jnp.sum(centred * centred, axis=0, keepdims=True)
    rows, factors = [], []
    for k in range(3):
        rows += [high[k : k + 1], low[k : k + 1]]
        own = centred[k : k + 1].astype(F32)
        factors += [own * (-256.0 * SIGMA), own * (-2.0 * SIGMA)]
    for k in range(4):
        rows.append((norm >> (8 * k)) & 255)
        factors.append(jnp.full((1, OWN), SIGMA * 256.0**k, F32))
    rows.append(jnp.ones((1, OWN), jnp.int32))
    factors.append(norm.astype(F32) * SIGMA)
    rows.append(jnp.zeros((FEATURES - len(rows), OWN), jnp.int32))
    factors.append(jnp.zeros((FEATURES - 11, OWN), F32))
    rows = jnp.concatenate(rows, axis=0).astype(F32)
    factors = jnp.concatenate(factors, axis=0)
    first = factors.astype(BF16).astype(F32)
    second = (factors - first).astype(BF16).astype(F32)
    third = factors - first - second
    stack = jnp.concatenate([first, second, third, jnp.zeros((128 - 3 * FEATURES, OWN), F32)], axis=0)
    return rows.astype(BF16), stack.T.astype(BF16)


def begin_values(squared):
    squared = jnp.maximum(squared, 1e-12)
    return squared, lax.rsqrt(squared)


def end_values(squared, inverse):
    turns = squared * inverse
    part = turns - ((turns + ROUNDER) - ROUNDER)
    q = part * part
    value = ((q + SINE[2]) * q + SINE[1]) * q + SINE[0]
    return (value * (part * inverse)).astype(BF16)


def body(
    pos_ref, rhs_ref, start_ref, sol_ref, res_ref,
    kt, v0, v1, v2, lt, phase0, phase1, kept0, kept1, acc, part_out, part_in, r0_ref, q0_ref, p1_ref, sum_a, sum_b,
    send_sems, recv_sems, sum_send, sum_recv, lt_sems,
):
    row, core = lax.axis_index("rows"), lax.axis_index("sub")
    z, rest = row // 16, lax.rem(row, 16)
    x, y = rest // 4, lax.rem(rest, 4)
    a, b = y + core * (x - y), x + core * (y - x)
    step_a, step_b = 1 + 3 * core, 4 - 3 * core

    def device(da=0, db=0, dz=0):
        place = lax.rem(z + dz, NZ) * 16 + lax.rem(a + da, NA) * step_a + lax.rem(b + db, NB) * step_b
        return (place, core)

    def partner(dx, dy, dz, ds):
        place = lax.rem(z + dz, NZ) * 16 + lax.rem(x + dx, 4) * 4 + lax.rem(y + dy, 4)
        return (place, 1 - core if ds else core)

    sibling = (row, 1 - core)

    barrier = pltpu.get_barrier_semaphore()
    greeted = 0
    for steps in SUM_SEM:
        pl.semaphore_signal(barrier, inc=1, device_id=partner(*steps), device_id_type=MESH)
        greeted += 1

    started = []

    def make_gather(number, field):
        def copy(name, src, dst, target):
            return pltpu.make_async_remote_copy(
                src_ref=src, dst_ref=dst,
                send_sem=send_sems.at[number, SEMS[name]], recv_sem=recv_sems.at[number, SEMS[name]],
                device_id=target, device_id_type=MESH,
            )

        def slot(da, db):
            return field.at[SLOT[(da, db)]]

        def z_copy(d):
            src = slot(0, 0)
            return copy(("z", d), src.at[:, 0:OWN], src.at[:, d * OWN : (d + 1) * OWN], device(dz=d))

        def b_copy(d):
            return copy(("b", d), slot(0, 0), slot(0, d), device(db=d))

        def b_half(half):
            cols = slice(half * (CHUNK // 2), (half + 1) * (CHUNK // 2))
            came = 1 if half == 0 else 3
            return copy(("b", 2, half), slot(0, came).at[:, cols], slot(0, 2).at[:, cols], device(db=came))

        def a_copy(d, db):
            if d == 2:
                came = 1 if db in (0, 1) else 3
                return copy(("a", 2, db), slot(came, db), slot(2, db), device(da=came))
            return copy(("a", d, db), slot(0, db), slot(d, db), device(da=d))

        def start(item):
            item.start()
            started.append(item)

        def begin():
            for d in (4, 3, 5, 2, 6, 1, 7):
                start(z_copy(d))

        def arrive(place):
            da, db = ORDER[place]
            if (da, db) == (0, 0):
                for d in range(1, NZ):
                    z_copy(d).wait_recv()
                start(b_copy(1))
                start(b_copy(3))
            elif da == 0:
                if db == 2:
                    b_half(0).wait_recv()
                    b_half(1).wait_recv()
                else:
                    b_copy(db).wait_recv()
                    start(b_half(0 if db == 1 else 1))
            else:
                a_copy(da, db).wait_recv()
                if (da == 1 and db in (0, 1)) or (da == 3 and db in (2, 3)):
                    start(a_copy(2, db))
            if da == 0:
                start(a_copy(1, db))
                start(a_copy(3, db))

        def whole():
            part_out[number] = acc[:, OWN:BOTH]
            item = copy("part", part_out.at[number], part_in.at[number], sibling)
            start(item)
            item.wait_recv()
            return SCALE * (acc[:, 0:OWN] + part_in[number])

        return begin, arrive, whole

    def make_sum(number, buffer):
        def copy(phase_index, steps):
            index = SUM_SEM[steps]
            return pltpu.make_async_remote_copy(
                src_ref=buffer.at[phase_index], dst_ref=buffer.at[3 + index],
                send_sem=sum_send.at[number, index], recv_sem=sum_recv.at[number, index],
                device_id=partner(*steps), device_id_type=MESH,
            )

        def begin(phase_index, value):
            buffer[phase_index] = value
            for steps in PHASES[phase_index]:
                item = copy(phase_index, steps)
                item.start()
                started.append(item)

        def finish(phase_index):
            value = buffer[phase_index]
            for steps in PHASES[phase_index]:
                copy(phase_index, steps).wait_recv()
                value = value + buffer[3 + SUM_SEM[steps]]
            return value

        return begin, finish

    rows, factors = features(pos_ref[...])
    v0[0, 0:RHS, 0:OWN] = start_ref[...].astype(BF16)
    v0[0, RHS : RHS + FEATURES, 0:OWN] = rows
    lt[0:OWN, :] = factors
    acc[...] = jnp.zeros_like(acc)
    kept1[...] = jnp.zeros_like(kept1)
    pl.semaphore_wait(barrier, greeted)

    begin, arrive, whole = make_gather(0, v0)
    begin()
    factors_copy = pltpu.make_async_remote_copy(
        src_ref=lt.at[0:OWN], dst_ref=lt.at[OWN:BOTH], send_sem=lt_sems.at[0], recv_sem=lt_sems.at[1],
        device_id=sibling, device_id_type=MESH,
    )
    factors_copy.start()
    started.append(factors_copy)

    def columns(place, quarter):
        return pl.ds(pl.multiple_of((place % 2) * HALF + quarter * QUARTER, QUARTER), QUARTER)

    def phases(buffer, place, quarter):
        part = v0[place // 2, RHS : RHS + FEATURES, columns(place, quarter)]
        buffer[...] = jnp.dot(
            lt[:, 0 : 3 * FEATURES], jnp.concatenate([part, part, part], axis=0), preferred_element_type=F32
        )

    def values(buffer, kept, place, quarter):
        blocks = [(slice(r, r + 16), slice(c, c + 256)) for c in range(0, QUARTER, 256) for r in range(0, BOTH, 16)]
        ready = begin_values(buffer[blocks[0]])
        for n, block in enumerate(blocks):
            now = ready
            if n + 1 < len(blocks):
                ready = begin_values(buffer[blocks[n + 1]])
            kept[block] = end_values(*now)
        kt[place // 2, :, columns(place, quarter)] = kept[...]

    def apply_quarter(kept, place, quarter):
        acc[...] += dot_nt(v0[place // 2, 0:RHS, columns(place, quarter)], kept[...])

    arrive(0)
    factors_copy.wait_recv()
    come = 1
    for first, last in zip((0,) + GROUPS, GROUPS):
        if first == 0:
            final = 1
        else:
            while come < min(last + 1, CHUNKS):
                arrive(come)
                come += 1
            final = min(2 * last, 2 * CHUNKS - 1)
        if first < 2:
            phases(phase0, 2 * first, 0)

        @pl.loop(2 * first, 2 * last)
        def _(place, final=final):
            phases(phase1, place, 1)
            apply_quarter(kept1, jnp.maximum(place - 1, 0), 1)
            values(phase0, kept0, place, 0)
            phases(phase0, jnp.minimum(place + 1, final), 0)
            apply_quarter(kept0, place, 0)
            values(phase1, kept1, place, 1)

    apply_quarter(kept1, 2 * CHUNKS - 1, 1)

    r0 = rhs_ref[...] - (whole() + start_ref[...])
    r0_ref[...] = r0

    v1[0, :, 0:OWN] = r0.astype(BF16)
    begin, arrive, whole = make_gather(1, v1)
    begin()
    acc[...] = jnp.zeros_like(acc)
    for place in range(CHUNKS):
        arrive(place)
        acc[...] += dot_nt(v1[place], kt[place])
    q0 = whole() + r0_ref[...]
    q0_ref[...] = q0

    v2[0, :, 0:OWN] = q0.astype(BF16)
    begin, arrive, whole = make_gather(2, v2)
    begin()
    sum_begin, sum_finish = make_sum(0, sum_a)
    r0 = r0_ref[...]
    curve = gram(r0, q0)
    curve = 0.5 * (curve + gram(q0, r0))
    sum_begin(0, jnp.concatenate([packed(gram(r0, r0)), packed(curve), packed(gram(q0, q0))], axis=0))
    acc[...] = jnp.zeros_like(acc)
    kept = {}
    for place in range(CHUNKS):
        arrive(place)
        acc[...] += dot_nt(v2[place], kt[place])
        if place in (1, 4):
            index = (1, 4).index(place)
            sum_begin(index + 1, sum_finish(index))
        if place == 11:
            total = sum_finish(2)
            g00, g01, g11 = unpacked(total[0:8]), unpacked(total[8:16]), unpacked(total[16:24])
            identity = (lax.broadcasted_iota(jnp.int32, (RHS, RHS), 0) == lax.broadcasted_iota(jnp.int32, (RHS, RHS), 1)).astype(F32)
            step0, inverse0 = solve((g01, g00), (g00, identity))
            back = jnp.dot(g01, step0, precision=HIGHEST, preferred_element_type=F32)
            bent = jnp.dot(g11, step0, precision=HIGHEST, preferred_element_type=F32)
            norm1 = g00 - back - dot_tn(step0, g01) + dot_tn(step0, bent)
            correction = jnp.dot(inverse0, norm1, precision=HIGHEST, preferred_element_type=F32)
            r0, q0 = r0_ref[...], q0_ref[...]
            r1 = r0 - dot_tn(step0, q0)
            res_ref[...] = r1
            sol_ref[...] = start_ref[...] + dot_tn(step0, r0)
            p1_ref[...] = r1 + dot_tn(correction, r0)
            r0_ref[...] = q0 + dot_tn(correction, q0)
            kept["step0"], kept["norm1"] = step0, norm1
    image = whole() + q0_ref[...]
    q1 = r0_ref[...] - dot_tn(kept["step0"], image)
    p1 = p1_ref[...]
    sum_begin, sum_finish = make_sum(1, sum_b)
    curve = 0.5 * (gram(p1, q1) + gram(q1, p1))
    sum_begin(0, packed(curve))
    for index in range(2):
        sum_begin(index + 1, sum_finish(index))
    (step1,) = solve((unpacked(sum_finish(2)), kept["norm1"]))
    sol_ref[...] += dot_tn(step1, p1)
    res_ref[...] -= dot_tn(step1, q1)

    for item in started:
        item.wait_send()


def shards(positions, right_side, start_guess):
    full = pl.BlockSpec(memory_space=pltpu.VMEM)
    shape = jax.ShapeDtypeStruct((RHS, OWN), F32)
    return pl.pallas_call(
        body,
        out_shape=(shape, shape),
        in_specs=[full] * 3,
        out_specs=(full, full),
        scratch_shapes=[
            pltpu.VMEM((CHUNKS, BOTH, CHUNK), BF16),
            pltpu.VMEM((CHUNKS, RHS + FEATURES, CHUNK), BF16),
            pltpu.VMEM((CHUNKS, RHS, CHUNK), BF16),
            pltpu.VMEM((CHUNKS, RHS, CHUNK), BF16),
            pltpu.VMEM((BOTH, 128), BF16),
            pltpu.VMEM((BOTH, QUARTER), F32),
            pltpu.VMEM((BOTH, QUARTER), F32),
            pltpu.VMEM((BOTH, QUARTER), BF16),
            pltpu.VMEM((BOTH, QUARTER), BF16),
            pltpu.VMEM((RHS, BOTH), F32),
            pltpu.VMEM((3, RHS, OWN), F32),
            pltpu.VMEM((3, RHS, OWN), F32),
            pltpu.VMEM((RHS, OWN), F32),
            pltpu.VMEM((RHS, OWN), F32),
            pltpu.VMEM((RHS, OWN), F32),
            pltpu.VMEM((3 + N_SUM, 24, 128), F32),
            pltpu.VMEM((3 + N_SUM, 8, 128), F32),
            pltpu.SemaphoreType.DMA((3, N_SEMS)),
            pltpu.SemaphoreType.DMA((3, N_SEMS)),
            pltpu.SemaphoreType.DMA((2, N_SUM)),
            pltpu.SemaphoreType.DMA((2, N_SUM)),
            pltpu.SemaphoreType.DMA((2,)),
        ],
        compiler_params=pltpu.CompilerParams(collective_id=0, has_side_effects=True, vmem_limit_bytes=60 * 1024 * 1024),
        name="block_cg",
    )(positions, right_side, start_guess)


def solution(mesh):
    placed = P(None, ("rows", "sub"))
    return jax.shard_map(shards, mesh=mesh, in_specs=(placed,) * 3, out_specs=(placed,) * 2, check_vma=False)
```

```python
import jax
import jax.numpy as jnp
from jax import lax
from jax.experimental import pallas as pl
from jax.experimental.pallas import tpu as pltpu
from jax.sharding import PartitionSpec as P

MESH = pl.DeviceIdType.MESH
F32, BF16 = jnp.float32, jnp.bfloat16
HIGHEST = lax.Precision.HIGHEST

RHS = 32
OWN = 256
CHUNK = 2048
HALF = CHUNK // 2
QUARTER = CHUNK // 4
BOTH = 2 * OWN
FEATURES = 16
NZ, NA, NB = 8, 4, 4

SIGMA = (0.009 / (2.0 * 3.141592653589793)) ** 2
SCALE = -1.0 / 0.11181640625
SINE = (-0.1117412088270527, 0.7314446032490506, -1.3877725895638588)
ROUNDER = 12582912.0

ORDER = ((0, 0), (0, 1), (0, 3), (0, 2), (1, 0), (3, 0), (1, 1), (3, 1), (3, 3), (1, 3), (3, 2), (1, 2), (2, 0), (2, 3), (2, 1), (2, 2))
SLOT = {key: place for place, key in enumerate(ORDER)}
CHUNKS = len(ORDER)
GROUPS = (1, 2, 3, 5, 8, 12, 16)

SEMS = {}
for _name in (
    [("z", d) for d in range(1, NZ)]
    + [("b", 1), ("b", 3), ("b", 2, 0), ("b", 2, 1)]
    + [("a", d, db) for d in (1, 2, 3) for db in range(NB)]
    + ["part"]
):
    SEMS[_name] = len(SEMS)
N_SEMS = len(SEMS)
PHASES = (
    [(0, 0, d, 0) for d in range(1, NZ)],
    [(d, 0, 0, s) for d in range(4) for s in range(2) if d + s],
    [(0, d, 0, 0) for d in range(1, 4)],
)
SUM_SEM = {}
for _phase in PHASES:
    for _steps in _phase:
        SUM_SEM[_steps] = len(SUM_SEM)
N_SUM = len(SUM_SEM)


def dot_nt(left, right, precision=None):
    return lax.dot_general(left, right, (((1,), (1,)), ((), ())), precision=precision, preferred_element_type=F32)


def dot_tn(left, right, precision=HIGHEST):
    return lax.dot_general(left, right, (((0,), (0,)), ((), ())), precision=precision, preferred_element_type=F32)


def gram(left, right):
    return dot_nt(left, right, HIGHEST)


def packed(square):
    return jnp.concatenate([square[8 * k : 8 * k + 8] for k in range(4)], axis=1)


def unpacked(rows):
    return jnp.concatenate([rows[:, 32 * k : 32 * k + 32] for k in range(4)], axis=0)


def begin_solve(matrix, targets):
    return jnp.concatenate([matrix, targets], axis=1) * (1.0 / jnp.max(matrix, axis=(0, 1), keepdims=True))


def solve_steps(work, first, last):
    where = lax.broadcasted_iota(jnp.int32, (RHS, 1), 0)
    for k in range(first, last, 2):
        for index, both in enumerate(work):
            top, low = both[k : k + 1, :], both[k + 1 : k + 2, :]
            a, b = top[:, k : k + 1], top[:, k + 1 : k + 2]
            c, d = low[:, k : k + 1], low[:, k + 1 : k + 2]
            inverse = 1.0 / (a * d - b * c)
            top, low = (d * inverse) * top - (b * inverse) * low, (a * inverse) * low - (c * inverse) * top
            rest = both - both[:, k : k + 1] * top - both[:, k + 1 : k + 2] * low
            work[index] = jnp.where(where == k, top, jnp.where(where == k + 1, low, rest))


def dot_nn(left, right):
    return jnp.dot(left, right, precision=HIGHEST, preferred_element_type=F32)


def features(positions):
    centred = positions - 10000
    high = (centred + 64) >> 7
    low = centred - high * 128
    norm = jnp.sum(centred * centred, axis=0, keepdims=True)
    rows, factors = [], []
    for k in range(3):
        rows += [high[k : k + 1], low[k : k + 1]]
        own = centred[k : k + 1].astype(F32)
        factors += [own * (-256.0 * SIGMA), own * (-2.0 * SIGMA)]
    for k in range(4):
        rows.append((norm >> (8 * k)) & 255)
        factors.append(jnp.full((1, OWN), SIGMA * 256.0**k, F32))
    rows.append(jnp.ones((1, OWN), jnp.int32))
    factors.append(norm.astype(F32) * SIGMA)
    rows.append(jnp.zeros((FEATURES - len(rows), OWN), jnp.int32))
    factors.append(jnp.zeros((FEATURES - 11, OWN), F32))
    rows = jnp.concatenate(rows, axis=0).astype(F32)
    factors = jnp.concatenate(factors, axis=0)
    first = factors.astype(BF16).astype(F32)
    second = (factors - first).astype(BF16).astype(F32)
    third = factors - first - second
    stack = jnp.concatenate([first, second, third, jnp.zeros((128 - 3 * FEATURES, OWN), F32)], axis=0)
    return rows.astype(BF16), stack.T.astype(BF16)


def begin_values(squared):
    squared = jnp.maximum(squared, 1e-12)
    return squared, lax.rsqrt(squared)


def end_values(squared, inverse):
    turns = squared * inverse
    part = turns - ((turns + ROUNDER) - ROUNDER)
    q = part * part
    value = ((q + SINE[2]) * q + SINE[1]) * q + SINE[0]
    return (value * (part * inverse)).astype(BF16)


def body(
    pos_ref, rhs_ref, start_ref, sol_ref, res_ref,
    kt, v0, v1, v2, lt, phase0, phase1, kept0, kept1, acc, part_out, part_in, r0_ref, q0_ref, sum_a, sum_b,
    send_sems, recv_sems, sum_send, sum_recv, lt_sems,
):
    row, core = lax.axis_index("rows"), lax.axis_index("sub")
    z, rest = row // 16, lax.rem(row, 16)
    x, y = rest // 4, lax.rem(rest, 4)
    a, b = y + core * (x - y), x + core * (y - x)
    step_a, step_b = 1 + 3 * core, 4 - 3 * core

    def device(da=0, db=0, dz=0):
        place = lax.rem(z + dz, NZ) * 16 + lax.rem(a + da, NA) * step_a + lax.rem(b + db, NB) * step_b
        return (place, core)

    def partner(dx, dy, dz, ds):
        place = lax.rem(z + dz, NZ) * 16 + lax.rem(x + dx, 4) * 4 + lax.rem(y + dy, 4)
        return (place, 1 - core if ds else core)

    sibling = (row, 1 - core)

    barrier = pltpu.get_barrier_semaphore()
    greeted = 0
    for steps in SUM_SEM:
        pl.semaphore_signal(barrier, inc=1, device_id=partner(*steps), device_id_type=MESH)
        greeted += 1

    started = []

    def make_gather(number, field):
        def copy(name, src, dst, target):
            return pltpu.make_async_remote_copy(
                src_ref=src, dst_ref=dst,
                send_sem=send_sems.at[number, SEMS[name]], recv_sem=recv_sems.at[number, SEMS[name]],
                device_id=target, device_id_type=MESH,
            )

        def slot(da, db):
            return field.at[SLOT[(da, db)]]

        def z_copy(d):
            src = slot(0, 0)
            return copy(("z", d), src.at[:, 0:OWN], src.at[:, d * OWN : (d + 1) * OWN], device(dz=d))

        def b_copy(d):
            return copy(("b", d), slot(0, 0), slot(0, d), device(db=d))

        def b_half(half):
            cols = slice(half * (CHUNK // 2), (half + 1) * (CHUNK // 2))
            came = 1 if half == 0 else 3
            return copy(("b", 2, half), slot(0, came).at[:, cols], slot(0, 2).at[:, cols], device(db=came))

        def a_copy(d, db):
            if d == 2:
                came = 1 if db in (0, 1) else 3
                return copy(("a", 2, db), slot(came, db), slot(2, db), device(da=came))
            return copy(("a", d, db), slot(0, db), slot(d, db), device(da=d))

        def start(item):
            item.start()
            started.append(item)

        def begin():
            for d in (4, 3, 5, 2, 6, 1, 7):
                start(z_copy(d))

        def arrive(place):
            da, db = ORDER[place]
            if (da, db) == (0, 0):
                for d in range(1, NZ):
                    z_copy(d).wait_recv()
                start(b_copy(1))
                start(b_copy(3))
            elif da == 0:
                if db == 2:
                    b_half(0).wait_recv()
                    b_half(1).wait_recv()
                else:
                    b_copy(db).wait_recv()
                    start(b_half(0 if db == 1 else 1))
            else:
                a_copy(da, db).wait_recv()
                if (da == 1 and db in (0, 1)) or (da == 3 and db in (2, 3)):
                    start(a_copy(2, db))
            if da == 0:
                start(a_copy(1, db))
                start(a_copy(3, db))

        def part():
            return copy("part", part_out.at[number], part_in.at[number], sibling)

        def share():
            part_out[number] = acc[:, OWN:BOTH]
            start(part())

        def whole():
            part().wait_recv()
            return SCALE * (acc[:, 0:OWN] + part_in[number])

        return begin, arrive, share, whole

    def make_sum(number, buffer):
        def copy(phase_index, steps):
            index = SUM_SEM[steps]
            return pltpu.make_async_remote_copy(
                src_ref=buffer.at[phase_index], dst_ref=buffer.at[3 + index],
                send_sem=sum_send.at[number, index], recv_sem=sum_recv.at[number, index],
                device_id=partner(*steps), device_id_type=MESH,
            )

        def begin(phase_index, value):
            buffer[phase_index] = value
            for steps in PHASES[phase_index]:
                item = copy(phase_index, steps)
                item.start()
                started.append(item)

        def finish(phase_index):
            value = buffer[phase_index]
            for steps in PHASES[phase_index]:
                copy(phase_index, steps).wait_recv()
                value = value + buffer[3 + SUM_SEM[steps]]
            return value

        return begin, finish

    rows, factors = features(pos_ref[...])
    v0[0, 0:RHS, 0:OWN] = start_ref[...].astype(BF16)
    v0[0, RHS : RHS + FEATURES, 0:OWN] = rows
    lt[0:OWN, :] = factors
    acc[...] = jnp.zeros_like(acc)
    kept1[...] = jnp.zeros_like(kept1)
    pl.semaphore_wait(barrier, greeted)

    begin, arrive, share, whole = make_gather(0, v0)
    begin()
    factors_copy = pltpu.make_async_remote_copy(
        src_ref=lt.at[0:OWN], dst_ref=lt.at[OWN:BOTH], send_sem=lt_sems.at[0], recv_sem=lt_sems.at[1],
        device_id=sibling, device_id_type=MESH,
    )
    factors_copy.start()
    started.append(factors_copy)

    def columns(place, quarter):
        return pl.ds(pl.multiple_of((place % 2) * HALF + quarter * QUARTER, QUARTER), QUARTER)

    def phases(buffer, place, quarter):
        part = v0[place // 2, RHS : RHS + FEATURES, columns(place, quarter)]
        buffer[...] = jnp.dot(
            lt[:, 0 : 3 * FEATURES], jnp.concatenate([part, part, part], axis=0), preferred_element_type=F32
        )

    def values(buffer, kept, place, quarter):
        blocks = [(slice(r, r + 16), slice(c, c + 256)) for c in range(0, QUARTER, 256) for r in range(0, BOTH, 16)]
        ready = begin_values(buffer[blocks[0]])
        for n, block in enumerate(blocks):
            now = ready
            if n + 1 < len(blocks):
                ready = begin_values(buffer[blocks[n + 1]])
            kept[block] = end_values(*now)
        kt[place // 2, :, columns(place, quarter)] = kept[...]

    def apply_quarter(kept, place, quarter):
        acc[...] += dot_nt(v0[place // 2, 0:RHS, columns(place, quarter)], kept[...])

    arrive(0)
    factors_copy.wait_recv()
    come = 1
    for first, last in zip((0,) + GROUPS, GROUPS):
        if first == 0:
            final = 1
        else:
            while come < min(last + 1, CHUNKS):
                arrive(come)
                come += 1
            final = min(2 * last, 2 * CHUNKS - 1)
        if first < 2:
            phases(phase0, 2 * first, 0)

        @pl.loop(2 * first, 2 * last)
        def _(place, final=final):
            phases(phase1, place, 1)
            apply_quarter(kept1, jnp.maximum(place - 1, 0), 1)
            values(phase0, kept0, place, 0)
            phases(phase0, jnp.minimum(place + 1, final), 0)
            apply_quarter(kept0, place, 0)
            values(phase1, kept1, place, 1)

    apply_quarter(kept1, 2 * CHUNKS - 1, 1)

    share()
    r0 = rhs_ref[...] - (whole() + start_ref[...])
    r0_ref[...] = r0

    v1[0, :, 0:OWN] = r0.astype(BF16)
    begin, arrive, share, whole = make_gather(1, v1)
    begin()
    acc[...] = jnp.zeros_like(acc)
    for place in range(CHUNKS):
        arrive(place)
        acc[...] += dot_nt(v1[place], kt[place])
    share()
    q0 = whole() + r0_ref[...]
    q0_ref[:, 0:OWN] = q0

    v2[0, :, 0:OWN] = q0.astype(BF16)
    begin, arrive, share, whole = make_gather(2, v2)
    begin()
    sum_begin, sum_finish = make_sum(0, sum_a)
    r0 = r0_ref[...]
    curve = gram(r0, q0)
    curve = 0.5 * (curve + gram(q0, r0))
    sum_begin(0, jnp.concatenate([packed(gram(r0, r0)), packed(curve), packed(gram(q0, q0))], axis=0))
    q0_copy = pltpu.make_async_remote_copy(
        src_ref=q0_ref.at[:, 0:OWN], dst_ref=q0_ref.at[:, OWN:BOTH], send_sem=lt_sems.at[2], recv_sem=lt_sems.at[3],
        device_id=sibling, device_id_type=MESH,
    )
    q0_copy.start()
    started.append(q0_copy)
    acc[...] = jnp.zeros_like(acc)
    for place in range(CHUNKS):
        arrive(place)
        acc[...] += dot_nt(v2[place], kt[place])
        if place in (1, 4):
            index = (1, 4).index(place)
            sum_begin(index + 1, sum_finish(index))
    q0_copy.wait_recv()

    chip_q0, product = q0_ref[...], acc[...]
    last_begin, last_finish = make_sum(1, sum_b)
    last_begin(0, packed((0.5 * SCALE) * (gram(chip_q0, product) + gram(product, chip_q0))))
    share()
    total = sum_finish(2)
    g00, g01, g11 = unpacked(total[0:8]), unpacked(total[8:16]), unpacked(total[16:24])
    identity = (lax.broadcasted_iota(jnp.int32, (RHS, RHS), 0) == lax.broadcasted_iota(jnp.int32, (RHS, RHS), 1)).astype(F32)
    work = [begin_solve(g01, g00), begin_solve(g00, identity)]
    solve_steps(work, 0, RHS // 2)
    last_begin(1, last_finish(0))
    solve_steps(work, RHS // 2, RHS)
    step0, inverse0 = work[0][:, RHS:], work[1][:, RHS:]
    back, bent = dot_nn(g01, step0), dot_nn(g11, step0)
    norm1 = g00 - back - dot_tn(step0, g01) + dot_tn(step0, bent)
    last_begin(2, last_finish(1))
    keep = identity + dot_nn(inverse0, norm1)
    cross = dot_tn(bent, keep)
    fixed = dot_tn(keep, dot_nn(g01, keep) - bent) - cross + dot_tn(step0, bent)
    r0, q0 = r0_ref[...], q0_ref[:, 0:OWN]
    image = whole() + q0
    turned = dot_tn(step0, q0)
    p1 = dot_tn(keep, r0) - turned
    q1 = dot_tn(keep, q0) - dot_tn(step0, image)
    sol_ref[...] = start_ref[...] + dot_tn(step0, r0)
    res_ref[...] = r0 - turned
    work = [begin_solve(fixed + dot_tn(step0, dot_nn(unpacked(last_finish(2)), step0)), norm1)]
    solve_steps(work, 0, RHS)
    step1 = work[0][:, RHS:]
    sol_ref[...] += dot_tn(step1, p1)
    res_ref[...] -= dot_tn(step1, q1)

    for item in started:
        item.wait_send()


def shards(positions, right_side, start_guess):
    full = pl.BlockSpec(memory_space=pltpu.VMEM)
    shape = jax.ShapeDtypeStruct((RHS, OWN), F32)
    return pl.pallas_call(
        body,
        out_shape=(shape, shape),
        in_specs=[full] * 3,
        out_specs=(full, full),
        scratch_shapes=[
            pltpu.VMEM((CHUNKS, BOTH, CHUNK), BF16),
            pltpu.VMEM((CHUNKS, RHS + FEATURES, CHUNK), BF16),
            pltpu.VMEM((CHUNKS, RHS, CHUNK), BF16),
            pltpu.VMEM((CHUNKS, RHS, CHUNK), BF16),
            pltpu.VMEM((BOTH, 128), BF16),
            pltpu.VMEM((BOTH, QUARTER), F32),
            pltpu.VMEM((BOTH, QUARTER), F32),
            pltpu.VMEM((BOTH, QUARTER), BF16),
            pltpu.VMEM((BOTH, QUARTER), BF16),
            pltpu.VMEM((RHS, BOTH), F32),
            pltpu.VMEM((3, RHS, OWN), F32),
            pltpu.VMEM((3, RHS, OWN), F32),
            pltpu.VMEM((RHS, OWN), F32),
            pltpu.VMEM((RHS, BOTH), F32),
            pltpu.VMEM((3 + N_SUM, 24, 128), F32),
            pltpu.VMEM((3 + N_SUM, 8, 128), F32),
            pltpu.SemaphoreType.DMA((3, N_SEMS)),
            pltpu.SemaphoreType.DMA((3, N_SEMS)),
            pltpu.SemaphoreType.DMA((2, N_SUM)),
            pltpu.SemaphoreType.DMA((2, N_SUM)),
            pltpu.SemaphoreType.DMA((4,)),
        ],
        compiler_params=pltpu.CompilerParams(collective_id=0, has_side_effects=True, vmem_limit_bytes=60 * 1024 * 1024),
        name="block_cg",
    )(positions, right_side, start_guess)


def solution(mesh):
    placed = P(None, ("rows", "sub"))
    return jax.shard_map(shards, mesh=mesh, in_specs=(placed,) * 3, out_specs=(placed,) * 2, check_vma=False)
```

```python
import functools

import jax
import jax.numpy as jnp
from jax import lax
from jax.experimental import pallas as pl
from jax.experimental.pallas import tpu as pltpu
from jax.sharding import PartitionSpec as P

MESH = pl.DeviceIdType.MESH
F32, BF16 = jnp.float32, jnp.bfloat16
HIGHEST = lax.Precision.HIGHEST

RHS = 32
OWN = 256
CHUNK = 2048
HALF = CHUNK // 2
QUARTER = CHUNK // 4
BOTH = 2 * OWN
FEATURES = 16
NZ, NA, NB = 8, 4, 4

SIGMA = (0.009 / (2.0 * 3.141592653589793)) ** 2
SCALE = -1.0 / 0.11181640625
SINE = (-0.1117412088270527, 0.7314446032490506, -1.3877725895638588)
ROUNDER = 12582912.0

ORDER = ((0, 0), (0, 1), (0, 3), (0, 2), (1, 0), (3, 0), (1, 1), (3, 1), (3, 3), (1, 3), (3, 2), (1, 2), (2, 0), (2, 3), (2, 1), (2, 2))
SLOT = {key: place for place, key in enumerate(ORDER)}
CHUNKS = len(ORDER)

SEMS = {}
for _name in (
    [("z", d) for d in range(1, NZ)]
    + [("b", 1), ("b", 3), ("b", 2, 0), ("b", 2, 1)]
    + [("a", d, db) for d in (1, 2, 3) for db in range(NB)]
    + ["part"]
):
    SEMS[_name] = len(SEMS)
N_SEMS = len(SEMS)
PHASES = (
    [(0, 0, d, 0) for d in range(1, NZ)],
    [(d, 0, 0, s) for d in range(4) for s in range(2) if d + s],
    [(0, d, 0, 0) for d in range(1, 4)],
)
SUM_SEM = {}
for _phase in PHASES:
    for _steps in _phase:
        SUM_SEM[_steps] = len(SUM_SEM)
N_SUM = len(SUM_SEM)


def dot_nt(left, right, precision=None):
    return lax.dot_general(left, right, (((1,), (1,)), ((), ())), precision=precision, preferred_element_type=F32)


def dot_tn(left, right, precision=HIGHEST):
    return lax.dot_general(left, right, (((0,), (0,)), ((), ())), precision=precision, preferred_element_type=F32)


def gram(left, right):
    return dot_nt(left, right, HIGHEST)


def packed(square):
    return jnp.concatenate([square[8 * k : 8 * k + 8] for k in range(4)], axis=1)


def unpacked(rows):
    return jnp.concatenate([rows[:, 32 * k : 32 * k + 32] for k in range(4)], axis=0)


def begin_solve(matrix, targets):
    return jnp.concatenate([matrix, targets], axis=1) * (1.0 / jnp.max(matrix, axis=(0, 1), keepdims=True))


def solve_steps(work, first, last):
    where = lax.broadcasted_iota(jnp.int32, (RHS, 1), 0)
    for k in range(first, last, 2):
        for index, both in enumerate(work):
            top, low = both[k : k + 1, :], both[k + 1 : k + 2, :]
            a, b = top[:, k : k + 1], top[:, k + 1 : k + 2]
            c, d = low[:, k : k + 1], low[:, k + 1 : k + 2]
            inverse = 1.0 / (a * d - b * c)
            top, low = (d * inverse) * top - (b * inverse) * low, (a * inverse) * low - (c * inverse) * top
            rest = both - both[:, k : k + 1] * top - both[:, k + 1 : k + 2] * low
            work[index] = jnp.where(where == k, top, jnp.where(where == k + 1, low, rest))


def dot_nn(left, right):
    return jnp.dot(left, right, precision=HIGHEST, preferred_element_type=F32)


def features(positions):
    centred = positions - 10000
    high = (centred + 64) >> 7
    low = centred - high * 128
    norm = jnp.sum(centred * centred, axis=0, keepdims=True)
    rows, factors = [], []
    for k in range(3):
        rows += [high[k : k + 1], low[k : k + 1]]
        own = centred[k : k + 1].astype(F32)
        factors += [own * (-256.0 * SIGMA), own * (-2.0 * SIGMA)]
    for k in range(4):
        rows.append((norm >> (8 * k)) & 255)
        factors.append(jnp.full((1, OWN), SIGMA * 256.0**k, F32))
    rows.append(jnp.ones((1, OWN), jnp.int32))
    factors.append(norm.astype(F32) * SIGMA)
    rows.append(jnp.zeros((FEATURES - len(rows), OWN), jnp.int32))
    factors.append(jnp.zeros((FEATURES - 11, OWN), F32))
    rows = jnp.concatenate(rows, axis=0).astype(F32)
    factors = jnp.concatenate(factors, axis=0)
    first = factors.astype(BF16).astype(F32)
    second = (factors - first).astype(BF16).astype(F32)
    third = factors - first - second
    stack = jnp.concatenate([first, second, third, jnp.zeros((128 - 3 * FEATURES, OWN), F32)], axis=0)
    return rows.astype(BF16), stack.T.astype(BF16)


def begin_values(squared):
    squared = jnp.maximum(squared, 1e-12)
    return squared, lax.rsqrt(squared)


def end_values(squared, inverse):
    turns = squared * inverse
    part = turns - ((turns + ROUNDER) - ROUNDER)
    q = part * part
    value = ((q + SINE[2]) * q + SINE[1]) * q + SINE[0]
    return (value * (part * inverse)).astype(BF16)


def body(
    pos_ref, rhs_ref, start_ref, sol_ref, res_ref,
    kt, v0, v1, v2, lt, phase0, phase1, kept0, kept1, acc, part_out, part_in, r0_ref, q0_ref, sum_a, sum_b,
    send_sems, recv_sems, sum_send, sum_recv, lt_sems,
):
    row, core = lax.axis_index("rows"), lax.axis_index("sub")
    z, rest = row // 16, lax.rem(row, 16)
    x, y = rest // 4, lax.rem(rest, 4)
    a, b = y + core * (x - y), x + core * (y - x)
    step_a, step_b = 1 + 3 * core, 4 - 3 * core

    def device(da=0, db=0, dz=0):
        place = lax.rem(z + dz, NZ) * 16 + lax.rem(a + da, NA) * step_a + lax.rem(b + db, NB) * step_b
        return (place, core)

    def partner(dx, dy, dz, ds):
        place = lax.rem(z + dz, NZ) * 16 + lax.rem(x + dx, 4) * 4 + lax.rem(y + dy, 4)
        return (place, 1 - core if ds else core)

    sibling = (row, 1 - core)

    barrier = pltpu.get_barrier_semaphore()
    greeted = 0
    for steps in SUM_SEM:
        pl.semaphore_signal(barrier, inc=1, device_id=partner(*steps), device_id_type=MESH)
        greeted += 1

    started = []

    def make_gather(number, field):
        def copy(name, src, dst, target):
            return pltpu.make_async_remote_copy(
                src_ref=src, dst_ref=dst,
                send_sem=send_sems.at[number, SEMS[name]], recv_sem=recv_sems.at[number, SEMS[name]],
                device_id=target, device_id_type=MESH,
            )

        def slot(da, db):
            return field.at[SLOT[(da, db)]]

        def z_copy(d):
            src = slot(0, 0)
            return copy(("z", d), src.at[:, 0:OWN], src.at[:, d * OWN : (d + 1) * OWN], device(dz=d))

        def b_copy(d):
            return copy(("b", d), slot(0, 0), slot(0, d), device(db=d))

        def b_half(half):
            cols = slice(half * (CHUNK // 2), (half + 1) * (CHUNK // 2))
            came = 1 if half == 0 else 3
            return copy(("b", 2, half), slot(0, came).at[:, cols], slot(0, 2).at[:, cols], device(db=came))

        def a_copy(d, db):
            if d == 2:
                came = 1 if db in (0, 1) else 3
                return copy(("a", 2, db), slot(came, db), slot(2, db), device(da=came))
            return copy(("a", d, db), slot(0, db), slot(d, db), device(da=d))

        def start(make, *which):
            make(*which).start()
            started.append(functools.partial(make, *which))

        def begin():
            for d in (4, 3, 5, 2, 6, 1, 7):
                start(z_copy, d)

        def arrive(place):
            da, db = ORDER[place]
            if (da, db) == (0, 0):
                for d in range(1, NZ):
                    z_copy(d).wait_recv()
                start(b_copy, 1)
                start(b_copy, 3)
            elif da == 0:
                if db == 2:
                    b_half(0).wait_recv()
                    b_half(1).wait_recv()
                else:
                    b_copy(db).wait_recv()
                    start(b_half, 0 if db == 1 else 1)
            else:
                a_copy(da, db).wait_recv()
                if (da == 1 and db in (0, 1)) or (da == 3 and db in (2, 3)):
                    start(a_copy, 2, db)
            if da == 0:
                start(a_copy, 1, db)
                start(a_copy, 3, db)

        def part():
            return copy("part", part_out.at[number], part_in.at[number], sibling)

        def share():
            part_out[number] = acc[:, OWN:BOTH]
            start(part)

        def whole():
            part().wait_recv()
            return SCALE * (acc[:, 0:OWN] + part_in[number])

        return begin, arrive, share, whole

    def make_sum(number, buffer):
        def copy(phase_index, steps):
            index = SUM_SEM[steps]
            return pltpu.make_async_remote_copy(
                src_ref=buffer.at[phase_index], dst_ref=buffer.at[3 + index],
                send_sem=sum_send.at[number, index], recv_sem=sum_recv.at[number, index],
                device_id=partner(*steps), device_id_type=MESH,
            )

        def begin(phase_index, value):
            buffer[phase_index] = value
            for steps in PHASES[phase_index]:
                copy(phase_index, steps).start()
                started.append(functools.partial(copy, phase_index, steps))

        def finish(phase_index):
            value = buffer[phase_index]
            for steps in PHASES[phase_index]:
                copy(phase_index, steps).wait_recv()
                value = value + buffer[3 + SUM_SEM[steps]]
            return value

        return begin, finish

    rows, factors = features(pos_ref[...])
    v0[0, 0:RHS, 0:OWN] = start_ref[...].astype(BF16)
    v0[0, RHS : RHS + FEATURES, 0:OWN] = rows
    lt[0:OWN, :] = factors
    acc[...] = jnp.zeros_like(acc)
    kept1[...] = jnp.zeros_like(kept1)
    pl.semaphore_wait(barrier, greeted)

    begin, arrive, share, whole = make_gather(0, v0)
    begin()
    factors_copy = functools.partial(
        pltpu.make_async_remote_copy,
        src_ref=lt.at[0:OWN], dst_ref=lt.at[OWN:BOTH], send_sem=lt_sems.at[0], recv_sem=lt_sems.at[1],
        device_id=sibling, device_id_type=MESH,
    )
    factors_copy().start()
    started.append(factors_copy)

    def columns(place, quarter):
        return pl.ds(pl.multiple_of((place % 2) * HALF + quarter * QUARTER, QUARTER), QUARTER)

    def phases(buffer, place, quarter):
        part = v0[place // 2, RHS : RHS + FEATURES, columns(place, quarter)]
        buffer[...] = jnp.dot(
            lt[:, 0 : 3 * FEATURES], jnp.concatenate([part, part, part], axis=0), preferred_element_type=F32
        )

    def values(buffer, kept, place, quarter):
        blocks = [(slice(r, r + 16), slice(c, c + 256)) for c in range(0, QUARTER, 256) for r in range(0, BOTH, 16)]
        ready = begin_values(buffer[blocks[0]])
        for n, block in enumerate(blocks):
            now = ready
            if n + 1 < len(blocks):
                ready = begin_values(buffer[blocks[n + 1]])
            kept[block] = end_values(*now)
        kt[place // 2, :, columns(place, quarter)] = kept[...]

    def apply_quarter(kept, place, quarter):
        acc[...] += dot_nt(v0[place // 2, 0:RHS, columns(place, quarter)], kept[...])

    def at(chunk, function, which):
        for place in which:
            pl.when(chunk == place)(functools.partial(function, place))

    def look_ahead(place):
        if place == 1:
            arrive(1)
        if place + 1 < CHUNKS:
            arrive(place + 1)
        if place == 1:
            phases(phase0, 2, 0)

    arrive(0)
    factors_copy().wait_recv()
    phases(phase0, 0, 0)

    @pl.loop(0, CHUNKS)
    def _(chunk):
        at(chunk, look_ahead, range(1, CHUNKS - 1))

        @pl.loop(2 * chunk, 2 * chunk + 2)
        def _(place):
            later = jnp.where(jnp.logical_or(place == 1, place == 2 * CHUNKS - 1), place, place + 1)
            phases(phase1, place, 1)
            apply_quarter(kept1, jnp.maximum(place - 1, 0), 1)
            values(phase0, kept0, place, 0)
            phases(phase0, later, 0)
            apply_quarter(kept0, place, 0)
            values(phase1, kept1, place, 1)

    apply_quarter(kept1, 2 * CHUNKS - 1, 1)

    share()
    r0 = rhs_ref[...] - (whole() + start_ref[...])
    r0_ref[...] = r0

    v1[0, :, 0:OWN] = r0.astype(BF16)
    begin, arrive, share, whole = make_gather(1, v1)
    begin()
    acc[...] = jnp.zeros_like(acc)

    @pl.loop(0, CHUNKS)
    def _(chunk):
        at(chunk, arrive, range(CHUNKS))
        acc[...] += dot_nt(v1[chunk], kt[chunk])

    share()
    q0 = whole() + r0_ref[...]
    q0_ref[:, 0:OWN] = q0

    v2[0, :, 0:OWN] = q0.astype(BF16)
    begin, arrive, share, whole = make_gather(2, v2)
    begin()
    sum_begin, sum_finish = make_sum(0, sum_a)
    r0 = r0_ref[...]
    curve = gram(r0, q0)
    curve = 0.5 * (curve + gram(q0, r0))
    sum_begin(0, jnp.concatenate([packed(gram(r0, r0)), packed(curve), packed(gram(q0, q0))], axis=0))
    q0_copy = functools.partial(
        pltpu.make_async_remote_copy,
        src_ref=q0_ref.at[:, 0:OWN], dst_ref=q0_ref.at[:, OWN:BOTH], send_sem=lt_sems.at[2], recv_sem=lt_sems.at[3],
        device_id=sibling, device_id_type=MESH,
    )
    q0_copy().start()
    started.append(q0_copy)
    acc[...] = jnp.zeros_like(acc)

    def arrive_and_sum(place):
        if place in (2, 5):
            index = (2, 5).index(place)
            sum_begin(index + 1, sum_finish(index))
        arrive(place)

    @pl.loop(0, CHUNKS)
    def _(chunk):
        at(chunk, arrive_and_sum, range(CHUNKS))
        acc[...] += dot_nt(v2[chunk], kt[chunk])

    q0_copy().wait_recv()

    chip_q0, product = q0_ref[...], acc[...]
    last_begin, last_finish = make_sum(1, sum_b)
    last_begin(0, packed((0.5 * SCALE) * (gram(chip_q0, product) + gram(product, chip_q0))))
    share()
    total = sum_finish(2)
    g00, g01, g11 = unpacked(total[0:8]), unpacked(total[8:16]), unpacked(total[16:24])
    identity = (lax.broadcasted_iota(jnp.int32, (RHS, RHS), 0) == lax.broadcasted_iota(jnp.int32, (RHS, RHS), 1)).astype(F32)
    work = [begin_solve(g01, g00), begin_solve(g00, identity)]
    solve_steps(work, 0, RHS // 2)
    last_begin(1, last_finish(0))
    solve_steps(work, RHS // 2, RHS)
    step0, inverse0 = work[0][:, RHS:], work[1][:, RHS:]
    back, bent = dot_nn(g01, step0), dot_nn(g11, step0)
    norm1 = g00 - back - dot_tn(step0, g01) + dot_tn(step0, bent)
    last_begin(2, last_finish(1))
    keep = identity + dot_nn(inverse0, norm1)
    cross = dot_tn(bent, keep)
    fixed = dot_tn(keep, dot_nn(g01, keep) - bent) - cross + dot_tn(step0, bent)
    r0, q0 = r0_ref[...], q0_ref[:, 0:OWN]
    image = whole() + q0
    turned = dot_tn(step0, q0)
    p1 = dot_tn(keep, r0) - turned
    q1 = dot_tn(keep, q0) - dot_tn(step0, image)
    sol_ref[...] = start_ref[...] + dot_tn(step0, r0)
    res_ref[...] = r0 - turned
    work = [begin_solve(fixed + dot_tn(step0, dot_nn(unpacked(last_finish(2)), step0)), norm1)]
    solve_steps(work, 0, RHS)
    step1 = work[0][:, RHS:]
    sol_ref[...] += dot_tn(step1, p1)
    res_ref[...] -= dot_tn(step1, q1)

    for make in started:
        make().wait_send()


def shards(positions, right_side, start_guess):
    full = pl.BlockSpec(memory_space=pltpu.VMEM)
    shape = jax.ShapeDtypeStruct((RHS, OWN), F32)
    return pl.pallas_call(
        body,
        out_shape=(shape, shape),
        in_specs=[full] * 3,
        out_specs=(full, full),
        scratch_shapes=[
            pltpu.VMEM((CHUNKS, BOTH, CHUNK), BF16),
            pltpu.VMEM((CHUNKS, RHS + FEATURES, CHUNK), BF16),
            pltpu.VMEM((CHUNKS, RHS, CHUNK), BF16),
            pltpu.VMEM((CHUNKS, RHS, CHUNK), BF16),
            pltpu.VMEM((BOTH, 128), BF16),
            pltpu.VMEM((BOTH, QUARTER), F32),
            pltpu.VMEM((BOTH, QUARTER), F32),
            pltpu.VMEM((BOTH, QUARTER), BF16),
            pltpu.VMEM((BOTH, QUARTER), BF16),
            pltpu.VMEM((RHS, BOTH), F32),
            pltpu.VMEM((3, RHS, OWN), F32),
            pltpu.VMEM((3, RHS, OWN), F32),
            pltpu.VMEM((RHS, OWN), F32),
            pltpu.VMEM((RHS, BOTH), F32),
            pltpu.VMEM((3 + N_SUM, 24, 128), F32),
            pltpu.VMEM((3 + N_SUM, 8, 128), F32),
            pltpu.SemaphoreType.DMA((3, N_SEMS)),
            pltpu.SemaphoreType.DMA((3, N_SEMS)),
            pltpu.SemaphoreType.DMA((2, N_SUM)),
            pltpu.SemaphoreType.DMA((2, N_SUM)),
            pltpu.SemaphoreType.DMA((4,)),
        ],
        compiler_params=pltpu.CompilerParams(collective_id=0, has_side_effects=True, vmem_limit_bytes=60 * 1024 * 1024),
        name="block_cg",
    )(positions, right_side, start_guess)


def solution(mesh):
    placed = P(None, ("rows", "sub"))
    return jax.shard_map(shards, mesh=mesh, in_specs=(placed,) * 3, out_specs=(placed,) * 2, check_vma=False)
```

```python
import functools

import jax
import jax.numpy as jnp
from jax import lax
from jax.experimental import pallas as pl
from jax.experimental.pallas import tpu as pltpu
from jax.sharding import PartitionSpec as P

MESH = pl.DeviceIdType.MESH
F32, BF16 = jnp.float32, jnp.bfloat16
HIGHEST = lax.Precision.HIGHEST

RHS = 32
OWN = 256
CHUNK = 2048
HALF = CHUNK // 2
QUARTER = CHUNK // 4
BOTH = 2 * OWN
FEATURES = 16
NZ, NA, NB = 8, 4, 4

SIGMA = (0.009 / (2.0 * 3.141592653589793)) ** 2
SCALE = -1.0 / 0.11181640625
SINE = (-0.1117412088270527, 0.7314446032490506, -1.3877725895638588)

ORDER = ((0, 0), (0, 1), (0, 3), (0, 2), (1, 0), (3, 0), (1, 1), (3, 1), (3, 3), (1, 3), (3, 2), (1, 2), (2, 0), (2, 3), (2, 1), (2, 2))
LOOK = (0, 2, 3, 4, 6, 7, 8, 10, 11, 11, 11, 11, 12, 13, 14, 15)
SLOT = {key: place for place, key in enumerate(ORDER)}
CHUNKS = len(ORDER)

SEMS = {}
for _name in (
    [("z", d) for d in range(1, NZ)]
    + [("b", 1), ("b", 3), ("b", 2, 0), ("b", 2, 1)]
    + [("a", d, db) for d in (1, 2, 3) for db in range(NB)]
    + ["part"]
):
    SEMS[_name] = len(SEMS)
N_SEMS = len(SEMS)
PHASES = (
    [(0, 0, d, 0) for d in range(1, NZ)],
    [(d, 0, 0, s) for d in range(4) for s in range(2) if d + s],
    [(0, d, 0, 0) for d in range(1, 4)],
)
SUM_SEM = {}
for _phase in PHASES:
    for _steps in _phase:
        SUM_SEM[_steps] = len(SUM_SEM)
N_SUM = len(SUM_SEM)


def dot_nt(left, right, precision=None):
    return lax.dot_general(left, right, (((1,), (1,)), ((), ())), precision=precision, preferred_element_type=F32)


def dot_tn(left, right, precision=HIGHEST):
    return lax.dot_general(left, right, (((0,), (0,)), ((), ())), precision=precision, preferred_element_type=F32)


def gram(left, right):
    return dot_nt(left, right, HIGHEST)


def packed(square):
    return jnp.concatenate([square[8 * k : 8 * k + 8] for k in range(4)], axis=1)


def unpacked(rows):
    return jnp.concatenate([rows[:, 32 * k : 32 * k + 32] for k in range(4)], axis=0)


def begin_solve(matrix, targets):
    return jnp.concatenate([matrix, targets], axis=1) * (1.0 / jnp.max(matrix, axis=(0, 1), keepdims=True))


def solve_steps(work, first, last):
    where = lax.broadcasted_iota(jnp.int32, (RHS, 1), 0)
    for k in range(first, last, 2):
        for index, both in enumerate(work):
            top, low = both[k : k + 1, :], both[k + 1 : k + 2, :]
            a, b = top[:, k : k + 1], top[:, k + 1 : k + 2]
            c, d = low[:, k : k + 1], low[:, k + 1 : k + 2]
            inverse = 1.0 / (a * d - b * c)
            top, low = (d * inverse) * top - (b * inverse) * low, (a * inverse) * low - (c * inverse) * top
            rest = both - both[:, k : k + 1] * top - both[:, k + 1 : k + 2] * low
            work[index] = jnp.where(where == k, top, jnp.where(where == k + 1, low, rest))


def dot_nn(left, right):
    return jnp.dot(left, right, precision=HIGHEST, preferred_element_type=F32)


def features(positions):
    centred = positions - 10000
    high = (centred + 64) >> 7
    low = centred - high * 128
    norm = jnp.sum(centred * centred, axis=0, keepdims=True)
    rows, factors = [], []
    for k in range(3):
        rows += [high[k : k + 1], low[k : k + 1]]
        own = centred[k : k + 1].astype(F32)
        factors += [own * (-256.0 * SIGMA), own * (-2.0 * SIGMA)]
    for k in range(4):
        rows.append((norm >> (8 * k)) & 255)
        factors.append(jnp.full((1, OWN), SIGMA * 256.0**k, F32))
    rows.append(jnp.ones((1, OWN), jnp.int32))
    factors.append(norm.astype(F32) * SIGMA)
    rows.append(jnp.zeros((FEATURES - len(rows), OWN), jnp.int32))
    factors.append(jnp.zeros((FEATURES - 11, OWN), F32))
    rows = jnp.concatenate(rows, axis=0).astype(F32)
    factors = jnp.concatenate(factors, axis=0)
    first = factors.astype(BF16).astype(F32)
    second = (factors - first).astype(BF16).astype(F32)
    third = factors - first - second
    stack = jnp.concatenate([first, second, third, jnp.zeros((128 - 3 * FEATURES, OWN), F32)], axis=0)
    return rows.astype(BF16), stack.T.astype(BF16)


def begin_values(squared):
    squared = jnp.maximum(squared, 1e-12)
    return squared, lax.rsqrt(squared)


def end_values(squared, inverse):
    turns = squared * inverse
    part = turns - jnp.round(turns)
    q = part * part
    value = ((q + SINE[2]) * q + SINE[1]) * q + SINE[0]
    return (value * (part * inverse)).astype(BF16)


def body(
    pos_ref, rhs_ref, start_ref, sol_ref, res_ref,
    kt, v0, v1, v2, lt, phase0, phase1, kept0, kept1, acc, part_out, part_in, r0_ref, q0_ref, sum_a, sum_b,
    send_sems, recv_sems, sum_send, sum_recv, lt_sems,
):
    row, core = lax.axis_index("rows"), lax.axis_index("sub")
    z, rest = row // 16, lax.rem(row, 16)
    x, y = rest // 4, lax.rem(rest, 4)
    a, b = y + core * (x - y), x + core * (y - x)
    step_a, step_b = 1 + 3 * core, 4 - 3 * core

    def device(da=0, db=0, dz=0):
        place = lax.rem(z + dz, NZ) * 16 + lax.rem(a + da, NA) * step_a + lax.rem(b + db, NB) * step_b
        return (place, core)

    def partner(dx, dy, dz, ds):
        place = lax.rem(z + dz, NZ) * 16 + lax.rem(x + dx, 4) * 4 + lax.rem(y + dy, 4)
        return (place, 1 - core if ds else core)

    sibling = (row, 1 - core)

    barrier = pltpu.get_barrier_semaphore()
    greeted = 0
    for steps in SUM_SEM:
        pl.semaphore_signal(barrier, inc=1, device_id=partner(*steps), device_id_type=MESH)
        greeted += 1

    started = []

    def make_gather(number, field):
        def copy(name, src, dst, target):
            return pltpu.make_async_remote_copy(
                src_ref=src, dst_ref=dst,
                send_sem=send_sems.at[number, SEMS[name]], recv_sem=recv_sems.at[number, SEMS[name]],
                device_id=target, device_id_type=MESH,
            )

        def slot(da, db):
            return field.at[SLOT[(da, db)]]

        def z_copy(d):
            src = slot(0, 0)
            return copy(("z", d), src.at[:, 0:OWN], src.at[:, d * OWN : (d + 1) * OWN], device(dz=d))

        def b_copy(d):
            return copy(("b", d), slot(0, 0), slot(0, d), device(db=d))

        def b_half(half):
            cols = slice(half * (CHUNK // 2), (half + 1) * (CHUNK // 2))
            came = 1 if half == 0 else 3
            return copy(("b", 2, half), slot(0, came).at[:, cols], slot(0, 2).at[:, cols], device(db=came))

        def a_copy(d, db):
            if d == 2:
                came = 1 if db in (0, 1) else 3
                return copy(("a", 2, db), slot(came, db), slot(2, db), device(da=came))
            return copy(("a", d, db), slot(0, db), slot(d, db), device(da=d))

        def start(make, *which):
            make(*which).start()
            started.append(functools.partial(make, *which))

        def begin():
            for d in (4, 3, 5, 2, 6, 1, 7):
                start(z_copy, d)

        def arrive(place):
            da, db = ORDER[place]
            if (da, db) == (0, 0):
                for d in range(1, NZ):
                    z_copy(d).wait_recv()
                start(b_copy, 1)
                start(b_copy, 3)
            elif da == 0:
                if db == 2:
                    b_half(0).wait_recv()
                    b_half(1).wait_recv()
                else:
                    b_copy(db).wait_recv()
                    start(b_half, 0 if db == 1 else 1)
            else:
                a_copy(da, db).wait_recv()
                if (da == 1 and db in (0, 1)) or (da == 3 and db in (2, 3)):
                    start(a_copy, 2, db)
            if da == 0:
                start(a_copy, 1, db)
                start(a_copy, 3, db)

        def part():
            return copy("part", part_out.at[number], part_in.at[number], sibling)

        def share():
            part_out[number] = acc[:, OWN:BOTH]
            start(part)

        def whole():
            part().wait_recv()
            return SCALE * (acc[:, 0:OWN] + part_in[number])

        return begin, arrive, share, whole

    def make_sum(number, buffer):
        def copy(phase_index, steps):
            index = SUM_SEM[steps]
            return pltpu.make_async_remote_copy(
                src_ref=buffer.at[phase_index], dst_ref=buffer.at[3 + index],
                send_sem=sum_send.at[number, index], recv_sem=sum_recv.at[number, index],
                device_id=partner(*steps), device_id_type=MESH,
            )

        def begin(phase_index, value):
            buffer[phase_index] = value
            for steps in PHASES[phase_index]:
                copy(phase_index, steps).start()
                started.append(functools.partial(copy, phase_index, steps))

        def finish(phase_index):
            value = buffer[phase_index]
            for steps in PHASES[phase_index]:
                copy(phase_index, steps).wait_recv()
                value = value + buffer[3 + SUM_SEM[steps]]
            return value

        return begin, finish

    rows, factors = features(pos_ref[...])
    v0[0, 0:RHS, 0:OWN] = start_ref[...].astype(BF16)
    v0[0, RHS : RHS + FEATURES, 0:OWN] = rows
    lt[0:OWN, :] = factors
    acc[...] = jnp.zeros_like(acc)
    kept1[...] = jnp.zeros_like(kept1)
    pl.semaphore_wait(barrier, greeted)

    begin, arrive, share, whole = make_gather(0, v0)
    begin()
    factors_copy = functools.partial(
        pltpu.make_async_remote_copy,
        src_ref=lt.at[0:OWN], dst_ref=lt.at[OWN:BOTH], send_sem=lt_sems.at[0], recv_sem=lt_sems.at[1],
        device_id=sibling, device_id_type=MESH,
    )
    factors_copy().start()
    started.append(factors_copy)

    def columns(place, quarter):
        return pl.ds(pl.multiple_of((place % 2) * HALF + quarter * QUARTER, QUARTER), QUARTER)

    def phases(buffer, place, quarter):
        part = v0[place // 2, RHS : RHS + FEATURES, columns(place, quarter)]
        buffer[...] = jnp.dot(
            lt[:, 0 : 3 * FEATURES], jnp.concatenate([part, part, part], axis=0), preferred_element_type=F32
        )

    def values(buffer, kept, place, quarter):
        blocks = [(slice(r, r + 16), slice(c, c + 256)) for c in range(0, QUARTER, 256) for r in range(0, BOTH, 16)]
        ready = begin_values(buffer[blocks[0]])
        for n, block in enumerate(blocks):
            now = ready
            if n + 1 < len(blocks):
                ready = begin_values(buffer[blocks[n + 1]])
            kept[block] = end_values(*now)
        kt[place // 2, :, columns(place, quarter)] = kept[...]

    def apply_quarter(kept, place, quarter):
        acc[...] += dot_nt(v0[place // 2, 0:RHS, columns(place, quarter)], kept[...])

    def at(chunk, function, which):
        for place in which:
            pl.when(chunk == place)(functools.partial(function, place))

    def look_ahead(place):
        if place == 1:
            arrive(1)
        if place + 1 < CHUNKS:
            arrive(place + 1)
        if place == 1:
            phases(phase0, 2, 0)

    arrive(0)
    factors_copy().wait_recv()
    phases(phase0, 0, 0)

    @pl.loop(0, CHUNKS)
    def _(chunk):
        at(chunk, look_ahead, range(1, CHUNKS - 1))

        @pl.loop(2 * chunk, 2 * chunk + 2)
        def _(place):
            later = jnp.where(jnp.logical_or(place == 1, place == 2 * CHUNKS - 1), place, place + 1)
            phases(phase1, place, 1)
            apply_quarter(kept1, jnp.maximum(place - 1, 0), 1)
            values(phase0, kept0, place, 0)
            phases(phase0, later, 0)
            apply_quarter(kept0, place, 0)
            values(phase1, kept1, place, 1)

    apply_quarter(kept1, 2 * CHUNKS - 1, 1)

    share()
    r0 = rhs_ref[...] - (whole() + start_ref[...])
    r0_ref[...] = r0

    def arrivals(place):
        for come in range(LOOK[place - 1] + 1 if place else 0, LOOK[place] + 1):
            arrive(come)

    v1[0, :, 0:OWN] = r0.astype(BF16)
    begin, arrive, share, whole = make_gather(1, v1)
    begin()
    acc[...] = jnp.zeros_like(acc)

    @pl.loop(0, CHUNKS)
    def _(chunk):
        at(chunk, arrivals, range(CHUNKS))
        acc[...] += dot_nt(v1[chunk], kt[chunk])

    share()
    q0 = whole() + r0_ref[...]
    q0_ref[:, 0:OWN] = q0

    v2[0, :, 0:OWN] = q0.astype(BF16)
    begin, arrive, share, whole = make_gather(2, v2)
    begin()
    sum_begin, sum_finish = make_sum(0, sum_a)
    r0 = r0_ref[...]
    curve = gram(r0, q0)
    curve = 0.5 * (curve + gram(q0, r0))
    sum_begin(0, jnp.concatenate([packed(gram(r0, r0)), packed(curve), packed(gram(q0, q0))], axis=0))
    q0_copy = functools.partial(
        pltpu.make_async_remote_copy,
        src_ref=q0_ref.at[:, 0:OWN], dst_ref=q0_ref.at[:, OWN:BOTH], send_sem=lt_sems.at[2], recv_sem=lt_sems.at[3],
        device_id=sibling, device_id_type=MESH,
    )
    q0_copy().start()
    started.append(q0_copy)
    acc[...] = jnp.zeros_like(acc)

    def arrive_and_sum(place):
        if place in (2, 5):
            index = (2, 5).index(place)
            sum_begin(index + 1, sum_finish(index))
        arrivals(place)

    @pl.loop(0, CHUNKS)
    def _(chunk):
        at(chunk, arrive_and_sum, range(CHUNKS))
        acc[...] += dot_nt(v2[chunk], kt[chunk])

    q0_copy().wait_recv()

    chip_q0, product = q0_ref[...], acc[...]
    last_begin, last_finish = make_sum(1, sum_b)
    last_begin(0, packed((0.5 * SCALE) * (gram(chip_q0, product) + gram(product, chip_q0))))
    share()
    total = sum_finish(2)
    g00, g01, g11 = unpacked(total[0:8]), unpacked(total[8:16]), unpacked(total[16:24])
    identity = (lax.broadcasted_iota(jnp.int32, (RHS, RHS), 0) == lax.broadcasted_iota(jnp.int32, (RHS, RHS), 1)).astype(F32)
    work = [begin_solve(g01, g00), begin_solve(g00, identity)]
    solve_steps(work, 0, RHS // 2)
    last_begin(1, last_finish(0))
    solve_steps(work, RHS // 2, RHS)
    step0, inverse0 = work[0][:, RHS:], work[1][:, RHS:]
    back, bent = dot_nn(g01, step0), dot_nn(g11, step0)
    norm1 = g00 - back - dot_tn(step0, g01) + dot_tn(step0, bent)
    last_begin(2, last_finish(1))
    keep = identity + dot_nn(inverse0, norm1)
    cross = dot_tn(bent, keep)
    fixed = dot_tn(keep, dot_nn(g01, keep) - bent) - cross + dot_tn(step0, bent)
    r0, q0 = r0_ref[...], q0_ref[:, 0:OWN]
    image = whole() + q0
    turned = dot_tn(step0, q0)
    p1 = dot_tn(keep, r0) - turned
    q1 = dot_tn(keep, q0) - dot_tn(step0, image)
    sol_ref[...] = start_ref[...] + dot_tn(step0, r0)
    res_ref[...] = r0 - turned
    work = [begin_solve(fixed + dot_tn(step0, dot_nn(unpacked(last_finish(2)), step0)), norm1)]
    solve_steps(work, 0, RHS)
    step1 = work[0][:, RHS:]
    sol_ref[...] += dot_tn(step1, p1)
    res_ref[...] -= dot_tn(step1, q1)

    for make in started:
        make().wait_send()


def shards(positions, right_side, start_guess):
    full = pl.BlockSpec(memory_space=pltpu.VMEM)
    shape = jax.ShapeDtypeStruct((RHS, OWN), F32)
    return pl.pallas_call(
        body,
        out_shape=(shape, shape),
        in_specs=[full] * 3,
        out_specs=(full, full),
        scratch_shapes=[
            pltpu.VMEM((CHUNKS, BOTH, CHUNK), BF16),
            pltpu.VMEM((CHUNKS, RHS + FEATURES, CHUNK), BF16),
            pltpu.VMEM((CHUNKS, RHS, CHUNK), BF16),
            pltpu.VMEM((CHUNKS, RHS, CHUNK), BF16),
            pltpu.VMEM((BOTH, 128), BF16),
            pltpu.VMEM((BOTH, QUARTER), F32),
            pltpu.VMEM((BOTH, QUARTER), F32),
            pltpu.VMEM((BOTH, QUARTER), BF16),
            pltpu.VMEM((BOTH, QUARTER), BF16),
            pltpu.VMEM((RHS, BOTH), F32),
            pltpu.VMEM((3, RHS, OWN), F32),
            pltpu.VMEM((3, RHS, OWN), F32),
            pltpu.VMEM((RHS, OWN), F32),
            pltpu.VMEM((RHS, BOTH), F32),
            pltpu.VMEM((3 + N_SUM, 24, 128), F32),
            pltpu.VMEM((3 + N_SUM, 8, 128), F32),
            pltpu.SemaphoreType.DMA((3, N_SEMS)),
            pltpu.SemaphoreType.DMA((3, N_SEMS)),
            pltpu.SemaphoreType.DMA((2, N_SUM)),
            pltpu.SemaphoreType.DMA((2, N_SUM)),
            pltpu.SemaphoreType.DMA((4,)),
        ],
        compiler_params=pltpu.CompilerParams(collective_id=0, has_side_effects=True, vmem_limit_bytes=60 * 1024 * 1024),
        name="block_cg",
    )(positions, right_side, start_guess)


def solution(mesh):
    placed = P(None, ("rows", "sub"))
    return jax.shard_map(shards, mesh=mesh, in_specs=(placed,) * 3, out_specs=(placed,) * 2, check_vma=False)
```

```python
import functools

import jax
import jax.numpy as jnp
from jax import lax
from jax.experimental import pallas as pl
from jax.experimental.pallas import tpu as pltpu
from jax.sharding import PartitionSpec as P

MESH = pl.DeviceIdType.MESH
F32, BF16 = jnp.float32, jnp.bfloat16
HIGHEST = lax.Precision.HIGHEST

RHS = 32
OWN = 256
CHUNK = 2048
HALF = CHUNK // 2
QUARTER = CHUNK // 4
BOTH = 2 * OWN
FEATURES = 16
NZ, NA, NB = 8, 4, 4

SIGMA = (0.009 / (2.0 * 3.141592653589793)) ** 2
SCALE = -1.0 / 0.11181640625
SINE = (-0.1117412088270527, 0.7314446032490506, -1.3877725895638588)
ROUNDER = 12582912.0

ORDER = ((0, 0), (0, 1), (0, 3), (0, 2), (1, 0), (3, 0), (1, 1), (3, 1), (3, 3), (1, 3), (3, 2), (1, 2), (2, 0), (2, 3), (2, 1), (2, 2))
SLOT = {key: place for place, key in enumerate(ORDER)}
CHUNKS = len(ORDER)

SEMS = {}
for _name in (
    [("z", d) for d in range(1, NZ)]
    + [("b", 1), ("b", 3), ("b", 2, 0), ("b", 2, 1)]
    + [("a", d, db) for d in (1, 2, 3) for db in range(NB)]
    + ["part"]
):
    SEMS[_name] = len(SEMS)
N_SEMS = len(SEMS)
PHASES = (
    [(0, 0, d, 0) for d in range(1, NZ)],
    [(d, 0, 0, s) for d in range(4) for s in range(2) if d + s],
    [(0, d, 0, 0) for d in range(1, 4)],
)
SUM_SEM = {}
for _phase in PHASES:
    for _steps in _phase:
        SUM_SEM[_steps] = len(SUM_SEM)
N_SUM = len(SUM_SEM)


def dot_nt(left, right, precision=None):
    return lax.dot_general(left, right, (((1,), (1,)), ((), ())), precision=precision, preferred_element_type=F32)


def dot_tn(left, right, precision=HIGHEST):
    return lax.dot_general(left, right, (((0,), (0,)), ((), ())), precision=precision, preferred_element_type=F32)


def gram(left, right):
    return dot_nt(left, right, HIGHEST)


def packed(square):
    return jnp.concatenate([square[8 * k : 8 * k + 8] for k in range(4)], axis=1)


def unpacked(rows):
    return jnp.concatenate([rows[:, 32 * k : 32 * k + 32] for k in range(4)], axis=0)


def begin_solve(matrix, targets):
    return jnp.concatenate([matrix, targets], axis=1) * (1.0 / jnp.max(matrix, axis=(0, 1), keepdims=True))


def solve_steps(work, first, last):
    where = lax.broadcasted_iota(jnp.int32, (RHS, 1), 0)
    for k in range(first, last, 2):
        for index, both in enumerate(work):
            top, low = both[k : k + 1, :], both[k + 1 : k + 2, :]
            a, b = top[:, k : k + 1], top[:, k + 1 : k + 2]
            c, d = low[:, k : k + 1], low[:, k + 1 : k + 2]
            inverse = 1.0 / (a * d - b * c)
            top, low = (d * inverse) * top - (b * inverse) * low, (a * inverse) * low - (c * inverse) * top
            rest = both - both[:, k : k + 1] * top - both[:, k + 1 : k + 2] * low
            work[index] = jnp.where(where == k, top, jnp.where(where == k + 1, low, rest))


def dot_nn(left, right):
    return jnp.dot(left, right, precision=HIGHEST, preferred_element_type=F32)


def features(positions):
    centred = positions - 10000
    high = (centred + 64) >> 7
    low = centred - high * 128
    norm = jnp.sum(centred * centred, axis=0, keepdims=True)
    rows, factors = [], []
    for k in range(3):
        rows += [high[k : k + 1], low[k : k + 1]]
        own = centred[k : k + 1].astype(F32)
        factors += [own * (-256.0 * SIGMA), own * (-2.0 * SIGMA)]
    for k in range(4):
        rows.append((norm >> (8 * k)) & 255)
        factors.append(jnp.full((1, OWN), SIGMA * 256.0**k, F32))
    rows.append(jnp.ones((1, OWN), jnp.int32))
    factors.append(norm.astype(F32) * SIGMA)
    rows.append(jnp.zeros((FEATURES - len(rows), OWN), jnp.int32))
    factors.append(jnp.zeros((FEATURES - 11, OWN), F32))
    rows = jnp.concatenate(rows, axis=0).astype(F32)
    factors = jnp.concatenate(factors, axis=0)
    first = factors.astype(BF16).astype(F32)
    second = (factors - first).astype(BF16).astype(F32)
    third = factors - first - second
    stack = jnp.concatenate([first, second, third, jnp.zeros((128 - 3 * FEATURES, OWN), F32)], axis=0)
    return rows.astype(BF16), stack.T.astype(BF16)


def begin_values(squared):
    squared = jnp.maximum(squared, 1e-12)
    return squared, lax.rsqrt(squared)


def end_values(squared, inverse):
    turns = squared * inverse
    part = turns - ((turns + ROUNDER) - ROUNDER)
    q = part * part
    value = ((q + SINE[2]) * q + SINE[1]) * q + SINE[0]
    return (value * (part * inverse)).astype(BF16)


def body(
    pos_ref, rhs_ref, start_ref, sol_ref, res_ref,
    kt, v0, v1, v2, lt, phase0, phase1, kept0, kept1, acc, acc_t, part_out, part_in, r0_ref, q0_ref, sum_a, sum_b,
    send_sems, recv_sems, sum_send, sum_recv, lt_sems,
):
    row, core = lax.axis_index("rows"), lax.axis_index("sub")
    z, rest = row // 16, lax.rem(row, 16)
    x, y = rest // 4, lax.rem(rest, 4)
    a, b = y + core * (x - y), x + core * (y - x)
    step_a, step_b = 1 + 3 * core, 4 - 3 * core

    def device(da=0, db=0, dz=0):
        place = lax.rem(z + dz, NZ) * 16 + lax.rem(a + da, NA) * step_a + lax.rem(b + db, NB) * step_b
        return (place, core)

    def partner(dx, dy, dz, ds):
        place = lax.rem(z + dz, NZ) * 16 + lax.rem(x + dx, 4) * 4 + lax.rem(y + dy, 4)
        return (place, 1 - core if ds else core)

    sibling = (row, 1 - core)

    barrier = pltpu.get_barrier_semaphore()
    greeted = 0
    for steps in SUM_SEM:
        pl.semaphore_signal(barrier, inc=1, device_id=partner(*steps), device_id_type=MESH)
        greeted += 1

    started = []

    def make_gather(number, field):
        def copy(name, src, dst, target):
            return pltpu.make_async_remote_copy(
                src_ref=src, dst_ref=dst,
                send_sem=send_sems.at[number, SEMS[name]], recv_sem=recv_sems.at[number, SEMS[name]],
                device_id=target, device_id_type=MESH,
            )

        def slot(da, db):
            return field.at[SLOT[(da, db)]]

        def z_copy(d):
            src = slot(0, 0)
            return copy(("z", d), src.at[:, 0:OWN], src.at[:, d * OWN : (d + 1) * OWN], device(dz=d))

        def b_copy(d):
            return copy(("b", d), slot(0, 0), slot(0, d), device(db=d))

        def b_half(half):
            cols = slice(half * (CHUNK // 2), (half + 1) * (CHUNK // 2))
            came = 1 if half == 0 else 3
            return copy(("b", 2, half), slot(0, came).at[:, cols], slot(0, 2).at[:, cols], device(db=came))

        def a_copy(d, db):
            if d == 2:
                came = 1 if db in (0, 1) else 3
                return copy(("a", 2, db), slot(came, db), slot(2, db), device(da=came))
            return copy(("a", d, db), slot(0, db), slot(d, db), device(da=d))

        def start(make, *which):
            make(*which).start()
            started.append(functools.partial(make, *which))

        def begin():
            for d in (4, 3, 5, 2, 6, 1, 7):
                start(z_copy, d)

        def arrive(place):
            da, db = ORDER[place]
            if (da, db) == (0, 0):
                for d in range(1, NZ):
                    z_copy(d).wait_recv()
                start(b_copy, 1)
                start(b_copy, 3)
            elif da == 0:
                if db == 2:
                    b_half(0).wait_recv()
                    b_half(1).wait_recv()
                else:
                    b_copy(db).wait_recv()
                    start(b_half, 0 if db == 1 else 1)
            else:
                a_copy(da, db).wait_recv()
                if (da == 1 and db in (0, 1)) or (da == 3 and db in (2, 3)):
                    start(a_copy, 2, db)
            if da == 0:
                start(a_copy, 1, db)
                start(a_copy, 3, db)

        def part():
            return copy("part", part_out.at[number], part_in.at[number], sibling)

        def share():
            part_out[number] = acc[:, OWN:BOTH]
            start(part)

        def whole():
            part().wait_recv()
            return SCALE * (acc[:, 0:OWN] + part_in[number])

        return begin, arrive, share, whole

    def make_sum(number, buffer):
        def copy(phase_index, steps):
            index = SUM_SEM[steps]
            return pltpu.make_async_remote_copy(
                src_ref=buffer.at[phase_index], dst_ref=buffer.at[3 + index],
                send_sem=sum_send.at[number, index], recv_sem=sum_recv.at[number, index],
                device_id=partner(*steps), device_id_type=MESH,
            )

        def begin(phase_index, value):
            buffer[phase_index] = value
            for steps in PHASES[phase_index]:
                copy(phase_index, steps).start()
                started.append(functools.partial(copy, phase_index, steps))

        def finish(phase_index):
            value = buffer[phase_index]
            for steps in PHASES[phase_index]:
                copy(phase_index, steps).wait_recv()
                value = value + buffer[3 + SUM_SEM[steps]]
            return value

        return begin, finish

    rows, factors = features(pos_ref[...])
    v0[0, 0:RHS, 0:OWN] = start_ref[...].astype(BF16)
    v0[0, RHS : RHS + FEATURES, 0:OWN] = rows
    lt[0:OWN, :] = factors
    acc[...] = jnp.zeros_like(acc)
    kept1[...] = jnp.zeros_like(kept1)
    pl.semaphore_wait(barrier, greeted)

    begin, arrive, share, whole = make_gather(0, v0)
    begin()
    factors_copy = functools.partial(
        pltpu.make_async_remote_copy,
        src_ref=lt.at[0:OWN], dst_ref=lt.at[OWN:BOTH], send_sem=lt_sems.at[0], recv_sem=lt_sems.at[1],
        device_id=sibling, device_id_type=MESH,
    )
    factors_copy().start()
    started.append(factors_copy)

    def columns(place, quarter):
        return pl.ds(pl.multiple_of((place % 2) * HALF + quarter * QUARTER, QUARTER), QUARTER)

    def phases(buffer, place, quarter):
        part = v0[place // 2, RHS : RHS + FEATURES, columns(place, quarter)]
        buffer[...] = jnp.dot(
            lt[:, 0 : 3 * FEATURES], jnp.concatenate([part, part, part], axis=0), preferred_element_type=F32
        )

    def values(buffer, kept, place, quarter):
        blocks = [(slice(r, r + 16), slice(c, c + 256)) for c in range(0, QUARTER, 256) for r in range(0, BOTH, 16)]
        ready = begin_values(buffer[blocks[0]])
        for n, block in enumerate(blocks):
            now = ready
            if n + 1 < len(blocks):
                ready = begin_values(buffer[blocks[n + 1]])
            kept[block] = end_values(*now)
        kt[place // 2, :, columns(place, quarter)] = kept[...]

    def apply_quarter(kept, place, quarter):
        acc[...] += dot_nt(v0[place // 2, 0:RHS, columns(place, quarter)], kept[...])

    def at(chunk, function, which):
        for place in which:
            pl.when(chunk == place)(functools.partial(function, place))

    def look_ahead(place):
        if place == 1:
            arrive(1)
        if place + 1 < CHUNKS:
            arrive(place + 1)
        if place == 1:
            phases(phase0, 2, 0)

    arrive(0)
    factors_copy().wait_recv()
    phases(phase0, 0, 0)

    @pl.loop(0, CHUNKS)
    def _(chunk):
        at(chunk, look_ahead, range(1, CHUNKS - 1))

        @pl.loop(2 * chunk, 2 * chunk + 2)
        def _(place):
            later = jnp.where(jnp.logical_or(place == 1, place == 2 * CHUNKS - 1), place, place + 1)
            phases(phase1, place, 1)
            apply_quarter(kept1, jnp.maximum(place - 1, 0), 1)
            values(phase0, kept0, place, 0)
            phases(phase0, later, 0)
            apply_quarter(kept0, place, 0)
            values(phase1, kept1, place, 1)

    apply_quarter(kept1, 2 * CHUNKS - 1, 1)

    share()
    r0 = rhs_ref[...] - (whole() + start_ref[...])
    r0_ref[...] = r0

    def apply_chunk(field, chunk):
        own_part = dot_nt(field[chunk], kt[chunk, 0:OWN])
        other_part = dot_nt(kt[chunk, OWN:BOTH], field[chunk])
        acc[:, 0:OWN] += own_part
        acc_t[...] += other_part

    v1[0, :, 0:OWN] = r0.astype(BF16)
    begin, arrive, share, whole = make_gather(1, v1)
    begin()
    acc[...] = jnp.zeros_like(acc)
    acc_t[...] = jnp.zeros_like(acc_t)

    @pl.loop(0, CHUNKS)
    def _(chunk):
        at(chunk, arrive, range(CHUNKS))
        apply_chunk(v1, chunk)

    acc[:, OWN:BOTH] = acc_t[...].T
    share()
    q0 = whole() + r0_ref[...]
    q0_ref[:, 0:OWN] = q0

    v2[0, :, 0:OWN] = q0.astype(BF16)
    begin, arrive, share, whole = make_gather(2, v2)
    begin()
    sum_begin, sum_finish = make_sum(0, sum_a)
    r0 = r0_ref[...]
    curve = gram(r0, q0)
    curve = 0.5 * (curve + gram(q0, r0))
    sum_begin(0, jnp.concatenate([packed(gram(r0, r0)), packed(curve), packed(gram(q0, q0))], axis=0))
    q0_copy = functools.partial(
        pltpu.make_async_remote_copy,
        src_ref=q0_ref.at[:, 0:OWN], dst_ref=q0_ref.at[:, OWN:BOTH], send_sem=lt_sems.at[2], recv_sem=lt_sems.at[3],
        device_id=sibling, device_id_type=MESH,
    )
    q0_copy().start()
    started.append(q0_copy)
    acc[...] = jnp.zeros_like(acc)
    acc_t[...] = jnp.zeros_like(acc_t)

    def arrive_and_sum(place):
        if place in (2, 5):
            index = (2, 5).index(place)
            sum_begin(index + 1, sum_finish(index))
        arrive(place)

    @pl.loop(0, CHUNKS)
    def _(chunk):
        at(chunk, arrive_and_sum, range(CHUNKS))
        apply_chunk(v2, chunk)

    q0_copy().wait_recv()
    acc[:, OWN:BOTH] = acc_t[...].T

    chip_q0, product = q0_ref[...], acc[...]
    last_begin, last_finish = make_sum(1, sum_b)
    last_begin(0, packed((0.5 * SCALE) * (gram(chip_q0, product) + gram(product, chip_q0))))
    share()
    total = sum_finish(2)
    g00, g01, g11 = unpacked(total[0:8]), unpacked(total[8:16]), unpacked(total[16:24])
    identity = (lax.broadcasted_iota(jnp.int32, (RHS, RHS), 0) == lax.broadcasted_iota(jnp.int32, (RHS, RHS), 1)).astype(F32)
    work = [begin_solve(g01, g00), begin_solve(g00, identity)]
    solve_steps(work, 0, RHS // 2)
    last_begin(1, last_finish(0))
    solve_steps(work, RHS // 2, RHS)
    step0, inverse0 = work[0][:, RHS:], work[1][:, RHS:]
    back, bent = dot_nn(g01, step0), dot_nn(g11, step0)
    norm1 = g00 - back - dot_tn(step0, g01) + dot_tn(step0, bent)
    last_begin(2, last_finish(1))
    keep = identity + dot_nn(inverse0, norm1)
    cross = dot_tn(bent, keep)
    fixed = dot_tn(keep, dot_nn(g01, keep) - bent) - cross + dot_tn(step0, bent)
    r0, q0 = r0_ref[...], q0_ref[:, 0:OWN]
    image = whole() + q0
    turned = dot_tn(step0, q0)
    p1 = dot_tn(keep, r0) - turned
    q1 = dot_tn(keep, q0) - dot_tn(step0, image)
    sol_ref[...] = start_ref[...] + dot_tn(step0, r0)
    res_ref[...] = r0 - turned
    work = [begin_solve(fixed + dot_tn(step0, dot_nn(unpacked(last_finish(2)), step0)), norm1)]
    solve_steps(work, 0, RHS)
    step1 = work[0][:, RHS:]
    sol_ref[...] += dot_tn(step1, p1)
    res_ref[...] -= dot_tn(step1, q1)

    for make in started:
        make().wait_send()


def shards(positions, right_side, start_guess):
    full = pl.BlockSpec(memory_space=pltpu.VMEM)
    shape = jax.ShapeDtypeStruct((RHS, OWN), F32)
    return pl.pallas_call(
        body,
        out_shape=(shape, shape),
        in_specs=[full] * 3,
        out_specs=(full, full),
        scratch_shapes=[
            pltpu.VMEM((CHUNKS, BOTH, CHUNK), BF16),
            pltpu.VMEM((CHUNKS, RHS + FEATURES, CHUNK), BF16),
            pltpu.VMEM((CHUNKS, RHS, CHUNK), BF16),
            pltpu.VMEM((CHUNKS, RHS, CHUNK), BF16),
            pltpu.VMEM((BOTH, 128), BF16),
            pltpu.VMEM((BOTH, QUARTER), F32),
            pltpu.VMEM((BOTH, QUARTER), F32),
            pltpu.VMEM((BOTH, QUARTER), BF16),
            pltpu.VMEM((BOTH, QUARTER), BF16),
            pltpu.VMEM((RHS, BOTH), F32),
            pltpu.VMEM((OWN, RHS), F32),
            pltpu.VMEM((3, RHS, OWN), F32),
            pltpu.VMEM((3, RHS, OWN), F32),
            pltpu.VMEM((RHS, OWN), F32),
            pltpu.VMEM((RHS, BOTH), F32),
            pltpu.VMEM((3 + N_SUM, 24, 128), F32),
            pltpu.VMEM((3 + N_SUM, 8, 128), F32),
            pltpu.SemaphoreType.DMA((3, N_SEMS)),
            pltpu.SemaphoreType.DMA((3, N_SEMS)),
            pltpu.SemaphoreType.DMA((2, N_SUM)),
            pltpu.SemaphoreType.DMA((2, N_SUM)),
            pltpu.SemaphoreType.DMA((4,)),
        ],
        compiler_params=pltpu.CompilerParams(collective_id=0, has_side_effects=True, vmem_limit_bytes=60 * 1024 * 1024),
        name="block_cg",
    )(positions, right_side, start_guess)


def solution(mesh):
    placed = P(None, ("rows", "sub"))
    return jax.shard_map(shards, mesh=mesh, in_specs=(placed,) * 3, out_specs=(placed,) * 2, check_vma=False)
```

```python
import jax
import jax.numpy as jnp
from jax import lax
from jax.experimental import pallas as pl
from jax.experimental.pallas import tpu as pltpu
from jax.sharding import PartitionSpec as P

MESH = pl.DeviceIdType.MESH
F32, BF16 = jnp.float32, jnp.bfloat16
HIGHEST = lax.Precision.HIGHEST

RHS = 32
OWN = 256
CHUNK = 2048
HALF = CHUNK // 2
QUARTER = CHUNK // 4
BOTH = 2 * OWN
FEATURES = 16
NZ, NA, NB = 8, 4, 4

SIGMA = (0.009 / (2.0 * 3.141592653589793)) ** 2
SCALE = -1.0 / 0.11181640625
SINE = (-0.1117412088270527, 0.7314446032490506, -1.3877725895638588)
ROUNDER = 12582912.0

ORDER = ((0, 0), (0, 1), (0, 3), (0, 2), (1, 0), (3, 0), (1, 1), (3, 1), (3, 3), (1, 3), (3, 2), (1, 2), (2, 0), (2, 3), (2, 1), (2, 2))
SLOT = {key: place for place, key in enumerate(ORDER)}
CHUNKS = len(ORDER)
GROUPS = (1, 2, 3, 5, 8, 12, 16)

SEMS = {}
for _name in (
    [("z", d) for d in range(1, NZ)]
    + [("b", 1), ("b", 3), ("b", 2, 0), ("b", 2, 1)]
    + [("a", d, db) for d in (1, 2, 3) for db in range(NB)]
    + ["part"]
):
    SEMS[_name] = len(SEMS)
N_SEMS = len(SEMS)
PHASES = (
    [(0, 0, d, 0) for d in range(1, NZ)],
    [(d, 0, 0, s) for d in range(4) for s in range(2) if d + s],
    [(0, d, 0, 0) for d in range(1, 4)],
)
SUM_SEM = {}
for _phase in PHASES:
    for _steps in _phase:
        SUM_SEM[_steps] = len(SUM_SEM)
N_SUM = len(SUM_SEM)


def dot_nt(left, right, precision=None):
    return lax.dot_general(left, right, (((1,), (1,)), ((), ())), precision=precision, preferred_element_type=F32)


def dot_tn(left, right, precision=HIGHEST):
    return lax.dot_general(left, right, (((0,), (0,)), ((), ())), precision=precision, preferred_element_type=F32)


def gram(left, right):
    return dot_nt(left, right, HIGHEST)


def packed(square):
    return jnp.concatenate([square[8 * k : 8 * k + 8] for k in range(4)], axis=1)


def unpacked(rows):
    return jnp.concatenate([rows[:, 32 * k : 32 * k + 32] for k in range(4)], axis=0)


def begin_solve(matrix, targets):
    return jnp.concatenate([matrix, targets], axis=1) * (1.0 / jnp.max(matrix, axis=(0, 1), keepdims=True))


def solve_steps(work, first, last):
    where = lax.broadcasted_iota(jnp.int32, (RHS, 1), 0)
    for k in range(first, last, 2):
        for index, both in enumerate(work):
            top, low = both[k : k + 1, :], both[k + 1 : k + 2, :]
            a, b = top[:, k : k + 1], top[:, k + 1 : k + 2]
            c, d = low[:, k : k + 1], low[:, k + 1 : k + 2]
            inverse = 1.0 / (a * d - b * c)
            top, low = (d * inverse) * top - (b * inverse) * low, (a * inverse) * low - (c * inverse) * top
            rest = both - both[:, k : k + 1] * top - both[:, k + 1 : k + 2] * low
            work[index] = jnp.where(where == k, top, jnp.where(where == k + 1, low, rest))


def dot_nn(left, right):
    return jnp.dot(left, right, precision=HIGHEST, preferred_element_type=F32)


def features(positions):
    centred = positions - 10000
    high = (centred + 64) >> 7
    low = centred - high * 128
    norm = jnp.sum(centred * centred, axis=0, keepdims=True)
    rows, factors = [], []
    for k in range(3):
        rows += [high[k : k + 1], low[k : k + 1]]
        own = centred[k : k + 1].astype(F32)
        factors += [own * (-256.0 * SIGMA), own * (-2.0 * SIGMA)]
    for k in range(4):
        rows.append((norm >> (8 * k)) & 255)
        factors.append(jnp.full((1, OWN), SIGMA * 256.0**k, F32))
    rows.append(jnp.ones((1, OWN), jnp.int32))
    factors.append(norm.astype(F32) * SIGMA)
    rows.append(jnp.zeros((FEATURES - len(rows), OWN), jnp.int32))
    factors.append(jnp.zeros((FEATURES - 11, OWN), F32))
    rows = jnp.concatenate(rows, axis=0).astype(F32)
    factors = jnp.concatenate(factors, axis=0)
    first = factors.astype(BF16).astype(F32)
    second = (factors - first).astype(BF16).astype(F32)
    third = factors - first - second
    stack = jnp.concatenate([first, second, third, jnp.zeros((128 - 3 * FEATURES, OWN), F32)], axis=0)
    return rows.astype(BF16), stack.T.astype(BF16)


def begin_values(squared):
    squared = jnp.maximum(squared, 1e-12)
    return squared, lax.rsqrt(squared)


def end_values(squared, inverse):
    turns = squared * inverse
    part = turns - ((turns + ROUNDER) - ROUNDER)
    q = part * part
    value = ((q + SINE[2]) * q + SINE[1]) * q + SINE[0]
    return (value * (part * inverse)).astype(BF16)


def body(
    pos_ref, rhs_ref, start_ref, sol_ref, res_ref,
    kt, v0, v1, v2, lt, phase0, phase1, kept0, kept1, acc, part_out, part_in, r0_ref, q0_ref, sum_a, sum_b,
    send_sems, recv_sems, sum_send, sum_recv, lt_sems,
):
    row, core = lax.axis_index("rows"), lax.axis_index("sub")
    z, rest = row // 16, lax.rem(row, 16)
    x, y = rest // 4, lax.rem(rest, 4)
    a, b = y + core * (x - y), x + core * (y - x)
    step_a, step_b = 1 + 3 * core, 4 - 3 * core

    def device(da=0, db=0, dz=0):
        place = lax.rem(z + dz, NZ) * 16 + lax.rem(a + da, NA) * step_a + lax.rem(b + db, NB) * step_b
        return (place, core)

    def partner(dx, dy, dz, ds):
        place = lax.rem(z + dz, NZ) * 16 + lax.rem(x + dx, 4) * 4 + lax.rem(y + dy, 4)
        return (place, 1 - core if ds else core)

    sibling = (row, 1 - core)

    barrier = pltpu.get_barrier_semaphore()
    greeted = 0
    for steps in SUM_SEM:
        pl.semaphore_signal(barrier, inc=1, device_id=partner(*steps), device_id_type=MESH)
        greeted += 1

    started = []

    def make_gather(number, field):
        def copy(name, src, dst, target):
            return pltpu.make_async_remote_copy(
                src_ref=src, dst_ref=dst,
                send_sem=send_sems.at[number, SEMS[name]], recv_sem=recv_sems.at[number, SEMS[name]],
                device_id=target, device_id_type=MESH,
            )

        def slot(da, db):
            return field.at[SLOT[(da, db)]]

        def z_copy(d):
            src = slot(0, 0)
            return copy(("z", d), src.at[:, 0:OWN], src.at[:, d * OWN : (d + 1) * OWN], device(dz=d))

        def b_copy(d):
            return copy(("b", d), slot(0, 0), slot(0, d), device(db=d))

        def b_half(half):
            cols = slice(half * (CHUNK // 2), (half + 1) * (CHUNK // 2))
            came = 1 if half == 0 else 3
            return copy(("b", 2, half), slot(0, came).at[:, cols], slot(0, 2).at[:, cols], device(db=came))

        def a_copy(d, db):
            if d == 2:
                came = 1 if db in (0, 1) else 3
                return copy(("a", 2, db), slot(came, db), slot(2, db), device(da=came))
            return copy(("a", d, db), slot(0, db), slot(d, db), device(da=d))

        def start(item):
            item.start()
            started.append(item)

        def begin():
            for d in (4, 3, 5, 2, 6, 1, 7):
                start(z_copy(d))

        def arrive(place):
            da, db = ORDER[place]
            if (da, db) == (0, 0):
                for d in range(1, NZ):
                    z_copy(d).wait_recv()
                start(b_copy(1))
                start(b_copy(3))
            elif da == 0:
                if db == 2:
                    b_half(0).wait_recv()
                    b_half(1).wait_recv()
                else:
                    b_copy(db).wait_recv()
                    start(b_half(0 if db == 1 else 1))
            else:
                a_copy(da, db).wait_recv()
                if (da == 1 and db in (0, 1)) or (da == 3 and db in (2, 3)):
                    start(a_copy(2, db))
            if da == 0:
                start(a_copy(1, db))
                start(a_copy(3, db))

        def part():
            return copy("part", part_out.at[number], part_in.at[number], sibling)

        def share():
            part_out[number] = acc[:, OWN:BOTH]
            start(part())

        def whole():
            part().wait_recv()
            return SCALE * (acc[:, 0:OWN] + part_in[number])

        return begin, arrive, share, whole

    def make_sum(number, buffer):
        def copy(phase_index, steps):
            index = SUM_SEM[steps]
            return pltpu.make_async_remote_copy(
                src_ref=buffer.at[phase_index], dst_ref=buffer.at[3 + index],
                send_sem=sum_send.at[number, index], recv_sem=sum_recv.at[number, index],
                device_id=partner(*steps), device_id_type=MESH,
            )

        def begin(phase_index, value):
            buffer[phase_index] = value
            for steps in PHASES[phase_index]:
                item = copy(phase_index, steps)
                item.start()
                started.append(item)

        def finish(phase_index):
            value = buffer[phase_index]
            for steps in PHASES[phase_index]:
                copy(phase_index, steps).wait_recv()
                value = value + buffer[3 + SUM_SEM[steps]]
            return value

        return begin, finish

    rows, factors = features(pos_ref[...])
    v0[0, 0:RHS, 0:OWN] = start_ref[...].astype(BF16)
    v0[0, RHS : RHS + FEATURES, 0:OWN] = rows
    lt[0:OWN, :] = factors
    acc[...] = jnp.zeros_like(acc)
    kept1[...] = jnp.zeros_like(kept1)
    pl.semaphore_wait(barrier, greeted)

    begin, arrive, share, whole = make_gather(0, v0)
    begin()
    factors_copy = pltpu.make_async_remote_copy(
        src_ref=lt.at[0:OWN], dst_ref=lt.at[OWN:BOTH], send_sem=lt_sems.at[0], recv_sem=lt_sems.at[1],
        device_id=sibling, device_id_type=MESH,
    )
    factors_copy.start()
    started.append(factors_copy)

    def columns(place, quarter):
        return pl.ds(pl.multiple_of((place % 2) * HALF + quarter * QUARTER, QUARTER), QUARTER)

    def phases(buffer, place, quarter):
        part = v0[place // 2, RHS : RHS + FEATURES, columns(place, quarter)]
        buffer[...] = jnp.dot(
            lt[...], jnp.concatenate([part] * (128 // FEATURES), axis=0), preferred_element_type=F32
        )

    def values(buffer, kept, place, quarter):
        blocks = [(slice(r, r + 16), slice(c, c + 256)) for c in range(0, QUARTER, 256) for r in range(0, BOTH, 16)]
        ready = begin_values(buffer[blocks[0]])
        for n, block in enumerate(blocks):
            now = ready
            if n + 1 < len(blocks):
                ready = begin_values(buffer[blocks[n + 1]])
            kept[block] = end_values(*now)
        kt[place // 2, :, columns(place, quarter)] = kept[...]

    def apply_quarter(kept, place, quarter):
        acc[...] += dot_nt(v0[place // 2, 0:RHS, columns(place, quarter)], kept[...])

    arrive(0)
    factors_copy.wait_recv()
    come = 1
    for first, last in zip((0,) + GROUPS, GROUPS):
        if first == 0:
            final = 1
        else:
            while come < min(last + 1, CHUNKS):
                arrive(come)
                come += 1
            final = min(2 * last, 2 * CHUNKS - 1)
        if first < 2:
            phases(phase0, 2 * first, 0)

        @pl.loop(2 * first, 2 * last)
        def _(place, final=final):
            phases(phase1, place, 1)
            apply_quarter(kept1, jnp.maximum(place - 1, 0), 1)
            values(phase0, kept0, place, 0)
            phases(phase0, jnp.minimum(place + 1, final), 0)
            apply_quarter(kept0, place, 0)
            values(phase1, kept1, place, 1)

    apply_quarter(kept1, 2 * CHUNKS - 1, 1)

    share()
    r0 = rhs_ref[...] - (whole() + start_ref[...])
    r0_ref[...] = r0

    v1[0, :, 0:OWN] = r0.astype(BF16)
    begin, arrive, share, whole = make_gather(1, v1)
    begin()
    acc[...] = jnp.zeros_like(acc)
    for place in range(CHUNKS):
        arrive(place)
        acc[...] += dot_nt(v1[place], kt[place])
    share()
    q0 = whole() + r0_ref[...]
    q0_ref[:, 0:OWN] = q0

    v2[0, :, 0:OWN] = q0.astype(BF16)
    begin, arrive, share, whole = make_gather(2, v2)
    begin()
    sum_begin, sum_finish = make_sum(0, sum_a)
    r0 = r0_ref[...]
    curve = gram(r0, q0)
    curve = 0.5 * (curve + gram(q0, r0))
    sum_begin(0, jnp.concatenate([packed(gram(r0, r0)), packed(curve), packed(gram(q0, q0))], axis=0))
    q0_copy = pltpu.make_async_remote_copy(
        src_ref=q0_ref.at[:, 0:OWN], dst_ref=q0_ref.at[:, OWN:BOTH], send_sem=lt_sems.at[2], recv_sem=lt_sems.at[3],
        device_id=sibling, device_id_type=MESH,
    )
    q0_copy.start()
    started.append(q0_copy)
    acc[...] = jnp.zeros_like(acc)
    for place in range(CHUNKS):
        arrive(place)
        acc[...] += dot_nt(v2[place], kt[place])
        if place in (1, 4):
            index = (1, 4).index(place)
            sum_begin(index + 1, sum_finish(index))
    q0_copy.wait_recv()

    chip_q0, product = q0_ref[...], acc[...]
    last_begin, last_finish = make_sum(1, sum_b)
    last_begin(0, packed((0.5 * SCALE) * (gram(chip_q0, product) + gram(product, chip_q0))))
    share()
    total = sum_finish(2)
    g00, g01, g11 = unpacked(total[0:8]), unpacked(total[8:16]), unpacked(total[16:24])
    identity = (lax.broadcasted_iota(jnp.int32, (RHS, RHS), 0) == lax.broadcasted_iota(jnp.int32, (RHS, RHS), 1)).astype(F32)
    work = [begin_solve(g01, g00), begin_solve(g00, identity)]
    solve_steps(work, 0, RHS // 2)
    last_begin(1, last_finish(0))
    solve_steps(work, RHS // 2, RHS)
    step0, inverse0 = work[0][:, RHS:], work[1][:, RHS:]
    back, bent = dot_nn(g01, step0), dot_nn(g11, step0)
    norm1 = g00 - back - dot_tn(step0, g01) + dot_tn(step0, bent)
    last_begin(2, last_finish(1))
    keep = identity + dot_nn(inverse0, norm1)
    cross = dot_tn(bent, keep)
    fixed = dot_tn(keep, dot_nn(g01, keep) - bent) - cross + dot_tn(step0, bent)
    r0, q0 = r0_ref[...], q0_ref[:, 0:OWN]
    image = whole() + q0
    turned = dot_tn(step0, q0)
    p1 = dot_tn(keep, r0) - turned
    q1 = dot_tn(keep, q0) - dot_tn(step0, image)
    sol_ref[...] = start_ref[...] + dot_tn(step0, r0)
    res_ref[...] = r0 - turned
    work = [begin_solve(fixed + dot_tn(step0, dot_nn(unpacked(last_finish(2)), step0)), norm1)]
    solve_steps(work, 0, RHS)
    step1 = work[0][:, RHS:]
    sol_ref[...] += dot_tn(step1, p1)
    res_ref[...] -= dot_tn(step1, q1)

    for item in started:
        item.wait_send()


def shards(positions, right_side, start_guess):
    full = pl.BlockSpec(memory_space=pltpu.VMEM)
    shape = jax.ShapeDtypeStruct((RHS, OWN), F32)
    return pl.pallas_call(
        body,
        out_shape=(shape, shape),
        in_specs=[full] * 3,
        out_specs=(full, full),
        scratch_shapes=[
            pltpu.VMEM((CHUNKS, BOTH, CHUNK), BF16),
            pltpu.VMEM((CHUNKS, RHS + FEATURES, CHUNK), BF16),
            pltpu.VMEM((CHUNKS, RHS, CHUNK), BF16),
            pltpu.VMEM((CHUNKS, RHS, CHUNK), BF16),
            pltpu.VMEM((BOTH, 128), BF16),
            pltpu.VMEM((BOTH, QUARTER), F32),
            pltpu.VMEM((BOTH, QUARTER), F32),
            pltpu.VMEM((BOTH, QUARTER), BF16),
            pltpu.VMEM((BOTH, QUARTER), BF16),
            pltpu.VMEM((RHS, BOTH), F32),
            pltpu.VMEM((3, RHS, OWN), F32),
            pltpu.VMEM((3, RHS, OWN), F32),
            pltpu.VMEM((RHS, OWN), F32),
            pltpu.VMEM((RHS, BOTH), F32),
            pltpu.VMEM((3 + N_SUM, 24, 128), F32),
            pltpu.VMEM((3 + N_SUM, 8, 128), F32),
            pltpu.SemaphoreType.DMA((3, N_SEMS)),
            pltpu.SemaphoreType.DMA((3, N_SEMS)),
            pltpu.SemaphoreType.DMA((2, N_SUM)),
            pltpu.SemaphoreType.DMA((2, N_SUM)),
            pltpu.SemaphoreType.DMA((4,)),
        ],
        compiler_params=pltpu.CompilerParams(collective_id=0, has_side_effects=True, vmem_limit_bytes=60 * 1024 * 1024),
        name="block_cg",
    )(positions, right_side, start_guess)


def solution(mesh):
    placed = P(None, ("rows", "sub"))
    return jax.shard_map(shards, mesh=mesh, in_specs=(placed,) * 3, out_specs=(placed,) * 2, check_vma=False)
```

```python
import functools

import jax
import jax.numpy as jnp
from jax import lax
from jax.experimental import pallas as pl
from jax.experimental.pallas import tpu as pltpu
from jax.sharding import PartitionSpec as P

MESH = pl.DeviceIdType.MESH
F32, BF16 = jnp.float32, jnp.bfloat16
HIGHEST = lax.Precision.HIGHEST

RHS = 32
OWN = 256
CHUNK = 2048
HALF = CHUNK // 2
QUARTER = CHUNK // 4
BOTH = 2 * OWN
FEATURES = 16
NZ, NA, NB = 8, 4, 4

ROUNDER = 12582912.0
SIGMA = (0.009 / (2.0 * 3.141592653589793)) ** 2
SCALE = -1.0 / 0.11181640625
SINE = (-0.1117412088270527, 0.7314446032490506, -1.3877725895638588)

ORDER = ((0, 0), (0, 1), (0, 3), (0, 2), (1, 0), (3, 0), (1, 1), (3, 1), (3, 3), (1, 3), (3, 2), (1, 2), (2, 0), (2, 3), (2, 1), (2, 2))
LOOK = (0, 2, 3, 4, 6, 7, 8, 10, 11, 11, 11, 11, 12, 13, 14, 15)
SLOT = {key: place for place, key in enumerate(ORDER)}
CHUNKS = len(ORDER)

SEMS = {}
for _name in (
    [("z", d) for d in range(1, NZ)]
    + [("b", 1), ("b", 3), ("b", 2, 0), ("b", 2, 1)]
    + [("a", d, db) for d in (1, 2, 3) for db in range(NB)]
    + ["part"]
):
    SEMS[_name] = len(SEMS)
N_SEMS = len(SEMS)
PHASES = (
    [(0, 0, d, 0) for d in range(1, NZ)],
    [(d, 0, 0, s) for d in range(4) for s in range(2) if d + s],
    [(0, d, 0, 0) for d in range(1, 4)],
)
SUM_SEM = {}
for _phase in PHASES:
    for _steps in _phase:
        SUM_SEM[_steps] = len(SUM_SEM)
N_SUM = len(SUM_SEM)


def dot_nt(left, right, precision=None):
    return lax.dot_general(left, right, (((1,), (1,)), ((), ())), precision=precision, preferred_element_type=F32)


def dot_tn(left, right, precision=HIGHEST):
    return lax.dot_general(left, right, (((0,), (0,)), ((), ())), precision=precision, preferred_element_type=F32)


def gram(left, right):
    return dot_nt(left, right, HIGHEST)


def packed(square):
    return jnp.concatenate([square[8 * k : 8 * k + 8] for k in range(4)], axis=1)


def unpacked(rows):
    return jnp.concatenate([rows[:, 32 * k : 32 * k + 32] for k in range(4)], axis=0)


def begin_solve(matrix, targets):
    return jnp.concatenate([matrix, targets], axis=1) * (1.0 / jnp.max(matrix, axis=(0, 1), keepdims=True))


def solve_steps(work, first, last):
    where = lax.broadcasted_iota(jnp.int32, (RHS, 1), 0)
    for k in range(first, last, 2):
        for index, both in enumerate(work):
            top, low = both[k : k + 1, :], both[k + 1 : k + 2, :]
            a, b = top[:, k : k + 1], top[:, k + 1 : k + 2]
            c, d = low[:, k : k + 1], low[:, k + 1 : k + 2]
            inverse = 1.0 / (a * d - b * c)
            top, low = (d * inverse) * top - (b * inverse) * low, (a * inverse) * low - (c * inverse) * top
            rest = both - both[:, k : k + 1] * top - both[:, k + 1 : k + 2] * low
            work[index] = jnp.where(where == k, top, jnp.where(where == k + 1, low, rest))


def dot_nn(left, right):
    return jnp.dot(left, right, precision=HIGHEST, preferred_element_type=F32)


def features(positions):
    centred = positions - 10000
    high = (centred + 64) >> 7
    low = centred - high * 128
    norm = jnp.sum(centred * centred, axis=0, keepdims=True)
    rows, factors = [], []
    for k in range(3):
        rows += [high[k : k + 1], low[k : k + 1]]
        own = centred[k : k + 1].astype(F32)
        factors += [own * (-256.0 * SIGMA), own * (-2.0 * SIGMA)]
    for k in range(4):
        rows.append((norm >> (8 * k)) & 255)
        factors.append(jnp.full((1, OWN), SIGMA * 256.0**k, F32))
    rows.append(jnp.ones((1, OWN), jnp.int32))
    factors.append(norm.astype(F32) * SIGMA)
    rows.append(jnp.zeros((FEATURES - len(rows), OWN), jnp.int32))
    factors.append(jnp.zeros((FEATURES - 11, OWN), F32))
    rows = jnp.concatenate(rows, axis=0).astype(F32)
    factors = jnp.concatenate(factors, axis=0)
    first = factors.astype(BF16).astype(F32)
    second = (factors - first).astype(BF16).astype(F32)
    third = factors - first - second
    stack = jnp.concatenate([first, second, third, jnp.zeros((128 - 3 * FEATURES, OWN), F32)], axis=0)
    return rows.astype(BF16), stack.T.astype(BF16)


def begin_values(squared):
    squared = jnp.maximum(squared, 1e-12)
    return squared, lax.rsqrt(squared)


def end_values(squared, inverse):
    turns = squared * inverse
    part = turns - ((turns + ROUNDER) - ROUNDER)
    q = part * part
    value = ((q + SINE[2]) * q + SINE[1]) * q + SINE[0]
    return (value * (part * inverse)).astype(BF16)


def body(
    pos_ref, rhs_ref, start_ref, sol_ref, res_ref,
    kt, v0, v1, v2, lt, phase0, phase1, kept0, kept1, acc, part_out, part_in, r0_ref, q0_ref, sum_a, sum_b,
    send_sems, recv_sems, sum_send, sum_recv, lt_sems,
):
    row, core = lax.axis_index("rows"), lax.axis_index("sub")
    z, rest = row // 16, lax.rem(row, 16)
    x, y = rest // 4, lax.rem(rest, 4)
    a, b = y + core * (x - y), x + core * (y - x)
    step_a, step_b = 1 + 3 * core, 4 - 3 * core

    def device(da=0, db=0, dz=0):
        place = lax.rem(z + dz, NZ) * 16 + lax.rem(a + da, NA) * step_a + lax.rem(b + db, NB) * step_b
        return (place, core)

    def partner(dx, dy, dz, ds):
        place = lax.rem(z + dz, NZ) * 16 + lax.rem(x + dx, 4) * 4 + lax.rem(y + dy, 4)
        return (place, 1 - core if ds else core)

    sibling = (row, 1 - core)

    barrier = pltpu.get_barrier_semaphore()
    greeted = 0
    for steps in SUM_SEM:
        pl.semaphore_signal(barrier, inc=1, device_id=partner(*steps), device_id_type=MESH)
        greeted += 1

    started = []

    def make_gather(number, field):
        def copy(name, src, dst, target):
            return pltpu.make_async_remote_copy(
                src_ref=src, dst_ref=dst,
                send_sem=send_sems.at[number, SEMS[name]], recv_sem=recv_sems.at[number, SEMS[name]],
                device_id=target, device_id_type=MESH,
            )

        def slot(da, db):
            return field.at[SLOT[(da, db)]]

        def z_copy(d):
            src = slot(0, 0)
            return copy(("z", d), src.at[:, 0:OWN], src.at[:, d * OWN : (d + 1) * OWN], device(dz=d))

        def b_copy(d):
            return copy(("b", d), slot(0, 0), slot(0, d), device(db=d))

        def b_half(half):
            cols = slice(half * (CHUNK // 2), (half + 1) * (CHUNK // 2))
            came = 1 if half == 0 else 3
            return copy(("b", 2, half), slot(0, came).at[:, cols], slot(0, 2).at[:, cols], device(db=came))

        def a_copy(d, db):
            if d == 2:
                came = 1 if db in (0, 1) else 3
                return copy(("a", 2, db), slot(came, db), slot(2, db), device(da=came))
            return copy(("a", d, db), slot(0, db), slot(d, db), device(da=d))

        def start(make, *which):
            make(*which).start()
            started.append(functools.partial(make, *which))

        def begin():
            for d in (4, 3, 5, 2, 6, 1, 7):
                start(z_copy, d)

        def arrive(place):
            da, db = ORDER[place]
            if (da, db) == (0, 0):
                for d in range(1, NZ):
                    z_copy(d).wait_recv()
                start(b_copy, 1)
                start(b_copy, 3)
            elif da == 0:
                if db == 2:
                    b_half(0).wait_recv()
                    b_half(1).wait_recv()
                else:
                    b_copy(db).wait_recv()
                    start(b_half, 0 if db == 1 else 1)
            else:
                a_copy(da, db).wait_recv()
                if (da == 1 and db in (0, 1)) or (da == 3 and db in (2, 3)):
                    start(a_copy, 2, db)
            if da == 0:
                start(a_copy, 1, db)
                start(a_copy, 3, db)

        def part():
            return copy("part", part_out.at[number], part_in.at[number], sibling)

        def share():
            part_out[number] = acc[:, OWN:BOTH]
            start(part)

        def whole():
            part().wait_recv()
            return SCALE * (acc[:, 0:OWN] + part_in[number])

        return begin, arrive, share, whole

    def make_sum(number, buffer):
        def copy(phase_index, steps):
            index = SUM_SEM[steps]
            return pltpu.make_async_remote_copy(
                src_ref=buffer.at[phase_index], dst_ref=buffer.at[3 + index],
                send_sem=sum_send.at[number, index], recv_sem=sum_recv.at[number, index],
                device_id=partner(*steps), device_id_type=MESH,
            )

        def begin(phase_index, value):
            buffer[phase_index] = value
            for steps in PHASES[phase_index]:
                copy(phase_index, steps).start()
                started.append(functools.partial(copy, phase_index, steps))

        def finish(phase_index):
            value = buffer[phase_index]
            for steps in PHASES[phase_index]:
                copy(phase_index, steps).wait_recv()
                value = value + buffer[3 + SUM_SEM[steps]]
            return value

        return begin, finish

    rows, factors = features(pos_ref[...])
    v0[0, 0:RHS, 0:OWN] = start_ref[...].astype(BF16)
    v0[0, RHS : RHS + FEATURES, 0:OWN] = rows
    lt[0:OWN, :] = factors
    acc[...] = jnp.zeros_like(acc)
    kept1[...] = jnp.zeros_like(kept1)
    pl.semaphore_wait(barrier, greeted)

    begin, arrive, share, whole = make_gather(0, v0)
    begin()
    factors_copy = functools.partial(
        pltpu.make_async_remote_copy,
        src_ref=lt.at[0:OWN], dst_ref=lt.at[OWN:BOTH], send_sem=lt_sems.at[0], recv_sem=lt_sems.at[1],
        device_id=sibling, device_id_type=MESH,
    )
    factors_copy().start()
    started.append(factors_copy)

    def columns(place, quarter):
        return pl.ds(pl.multiple_of((place % 2) * HALF + quarter * QUARTER, QUARTER), QUARTER)

    def phases(buffer, place, quarter):
        part = v0[place // 2, RHS : RHS + FEATURES, columns(place, quarter)]
        buffer[...] = jnp.dot(
            lt[:, 0 : 3 * FEATURES], jnp.concatenate([part, part, part], axis=0), preferred_element_type=F32
        )

    def values(buffer, kept, place, quarter):
        blocks = [(slice(r, r + 16), slice(c, c + 256)) for c in range(0, QUARTER, 256) for r in range(0, BOTH, 16)]
        ready = begin_values(buffer[blocks[0]])
        for n, block in enumerate(blocks):
            now = ready
            if n + 1 < len(blocks):
                ready = begin_values(buffer[blocks[n + 1]])
            kept[block] = end_values(*now)
        kt[place // 2, :, columns(place, quarter)] = kept[...]

    def apply_quarter(kept, place, quarter):
        acc[...] += dot_nt(v0[place // 2, 0:RHS, columns(place, quarter)], kept[...])

    def at(chunk, function, which):
        for place in which:
            pl.when(chunk == place)(functools.partial(function, place))

    def look_ahead(place):
        if place == 1:
            arrive(1)
        if place + 1 < CHUNKS:
            arrive(place + 1)
        if place == 1:
            phases(phase0, 2, 0)

    arrive(0)
    factors_copy().wait_recv()
    phases(phase0, 0, 0)

    @pl.loop(0, CHUNKS)
    def _(chunk):
        at(chunk, look_ahead, range(1, CHUNKS - 1))

        @pl.loop(2 * chunk, 2 * chunk + 2)
        def _(place):
            later = jnp.where(jnp.logical_or(place == 1, place == 2 * CHUNKS - 1), place, place + 1)
            phases(phase1, place, 1)
            apply_quarter(kept1, jnp.maximum(place - 1, 0), 1)
            values(phase0, kept0, place, 0)
            phases(phase0, later, 0)
            apply_quarter(kept0, place, 0)
            values(phase1, kept1, place, 1)

    apply_quarter(kept1, 2 * CHUNKS - 1, 1)

    share()
    r0 = rhs_ref[...] - (whole() + start_ref[...])
    r0_ref[...] = r0

    def arrivals(place):
        for come in range(LOOK[place - 1] + 1 if place else 0, LOOK[place] + 1):
            arrive(come)

    v1[0, :, 0:OWN] = r0.astype(BF16)
    begin, arrive, share, whole = make_gather(1, v1)
    begin()
    acc[...] = jnp.zeros_like(acc)

    @pl.loop(0, CHUNKS)
    def _(chunk):
        at(chunk, arrivals, range(CHUNKS))
        acc[...] += dot_nt(v1[chunk], kt[chunk])

    share()
    q0 = whole() + r0_ref[...]
    q0_ref[:, 0:OWN] = q0

    v2[0, :, 0:OWN] = q0.astype(BF16)
    begin, arrive, share, whole = make_gather(2, v2)
    begin()
    sum_begin, sum_finish = make_sum(0, sum_a)
    r0 = r0_ref[...]
    curve = gram(r0, q0)
    curve = 0.5 * (curve + gram(q0, r0))
    sum_begin(0, jnp.concatenate([packed(gram(r0, r0)), packed(curve), packed(gram(q0, q0))], axis=0))
    q0_copy = functools.partial(
        pltpu.make_async_remote_copy,
        src_ref=q0_ref.at[:, 0:OWN], dst_ref=q0_ref.at[:, OWN:BOTH], send_sem=lt_sems.at[2], recv_sem=lt_sems.at[3],
        device_id=sibling, device_id_type=MESH,
    )
    q0_copy().start()
    started.append(q0_copy)
    acc[...] = jnp.zeros_like(acc)

    def arrive_and_sum(place):
        if place in (2, 5):
            index = (2, 5).index(place)
            sum_begin(index + 1, sum_finish(index))
        arrivals(place)

    @pl.loop(0, CHUNKS)
    def _(chunk):
        at(chunk, arrive_and_sum, range(CHUNKS))
        acc[...] += dot_nt(v2[chunk], kt[chunk])

    q0_copy().wait_recv()

    chip_q0, product = q0_ref[...], acc[...]
    last_begin, last_finish = make_sum(1, sum_b)
    last_begin(0, packed((0.5 * SCALE) * (gram(chip_q0, product) + gram(product, chip_q0))))
    share()
    total = sum_finish(2)
    g00, g01, g11 = unpacked(total[0:8]), unpacked(total[8:16]), unpacked(total[16:24])
    identity = (lax.broadcasted_iota(jnp.int32, (RHS, RHS), 0) == lax.broadcasted_iota(jnp.int32, (RHS, RHS), 1)).astype(F32)
    work = [begin_solve(g01, g00), begin_solve(g00, identity)]
    solve_steps(work, 0, RHS // 2)
    last_begin(1, last_finish(0))
    solve_steps(work, RHS // 2, RHS)
    step0, inverse0 = work[0][:, RHS:], work[1][:, RHS:]
    back, bent = dot_nn(g01, step0), dot_nn(g11, step0)
    norm1 = g00 - back - dot_tn(step0, g01) + dot_tn(step0, bent)
    last_begin(2, last_finish(1))
    keep = identity + dot_nn(inverse0, norm1)
    cross = dot_tn(bent, keep)
    fixed = dot_tn(keep, dot_nn(g01, keep) - bent) - cross + dot_tn(step0, bent)
    r0, q0 = r0_ref[...], q0_ref[:, 0:OWN]
    image = whole() + q0
    turned = dot_tn(step0, q0)
    p1 = dot_tn(keep, r0) - turned
    q1 = dot_tn(keep, q0) - dot_tn(step0, image)
    sol_ref[...] = start_ref[...] + dot_tn(step0, r0)
    res_ref[...] = r0 - turned
    work = [begin_solve(fixed + dot_tn(step0, dot_nn(unpacked(last_finish(2)), step0)), norm1)]
    solve_steps(work, 0, RHS)
    step1 = work[0][:, RHS:]
    sol_ref[...] += dot_tn(step1, p1)
    res_ref[...] -= dot_tn(step1, q1)

    for make in started:
        make().wait_send()


def shards(positions, right_side, start_guess):
    full = pl.BlockSpec(memory_space=pltpu.VMEM)
    shape = jax.ShapeDtypeStruct((RHS, OWN), F32)
    return pl.pallas_call(
        body,
        out_shape=(shape, shape),
        in_specs=[full] * 3,
        out_specs=(full, full),
        scratch_shapes=[
            pltpu.VMEM((CHUNKS, BOTH, CHUNK), BF16),
            pltpu.VMEM((CHUNKS, RHS + FEATURES, CHUNK), BF16),
            pltpu.VMEM((CHUNKS, RHS, CHUNK), BF16),
            pltpu.VMEM((CHUNKS, RHS, CHUNK), BF16),
            pltpu.VMEM((BOTH, 128), BF16),
            pltpu.VMEM((BOTH, QUARTER), F32),
            pltpu.VMEM((BOTH, QUARTER), F32),
            pltpu.VMEM((BOTH, QUARTER), BF16),
            pltpu.VMEM((BOTH, QUARTER), BF16),
            pltpu.VMEM((RHS, BOTH), F32),
            pltpu.VMEM((3, RHS, OWN), F32),
            pltpu.VMEM((3, RHS, OWN), F32),
            pltpu.VMEM((RHS, OWN), F32),
            pltpu.VMEM((RHS, BOTH), F32),
            pltpu.VMEM((3 + N_SUM, 24, 128), F32),
            pltpu.VMEM((3 + N_SUM, 8, 128), F32),
            pltpu.SemaphoreType.DMA((3, N_SEMS)),
            pltpu.SemaphoreType.DMA((3, N_SEMS)),
            pltpu.SemaphoreType.DMA((2, N_SUM)),
            pltpu.SemaphoreType.DMA((2, N_SUM)),
            pltpu.SemaphoreType.DMA((4,)),
        ],
        compiler_params=pltpu.CompilerParams(collective_id=0, has_side_effects=True, vmem_limit_bytes=60 * 1024 * 1024),
        name="block_cg",
    )(positions, right_side, start_guess)


def solution(mesh):
    placed = P(None, ("rows", "sub"))
    return jax.shard_map(shards, mesh=mesh, in_specs=(placed,) * 3, out_specs=(placed,) * 2, check_vma=False)
```
